256 devices in a mesh: row: 32 (over z, y_lo, core), col: 8 (over x, y_hi).
Axes of the slice: x: 4, y: 4 (y_hi: 2, y_lo: 2; y = y_hi * 2 + y_lo), z: 8, core: 2. Of those that a mesh axis runs over, the one named last changes fastest.
Arguments:
- charges: bfloat16 [64, 1048576], P(None, ('row', 'col')), may hold values from -6 to 6
- points: float32 [3, 1048576], P(None, ('row', 'col')), may hold values from 0 to 128, as said below
- leaf_basis: bfloat16 [32, 1048576], P(None, ('row', 'col')), may hold values from -0.75 to 0.75
- transfer_one: bfloat16 [16384, 32, 32], P(('row', 'col')), may hold values from -0.5 to 0.5
- transfer_two: bfloat16 [2048, 32, 32], P(('row', 'col')), may hold values from -0.5 to 0.5
- couple_one: bfloat16 [2048, 12, 32, 32], P(('row', 'col')), may hold values from -0.3125 to 0.3125
- couple_two: bfloat16 [256, 16, 32, 32], P(('row', 'col')), may hold values from -0.25 to 0.25
- near_list: int32 [16384, 27], P(('row', 'col')), may hold values from -1 to 16383, as said below
- list_one: int32 [2048, 12], P(('row', 'col')), may hold values from -1 to 2047, as said below
- list_two: int32 [256, 16], P(('row', 'col')), may hold values from 0 to 255
Outputs:
- potential: bfloat16 [64, 1048576], P(None, ('row', 'col'))
The draws below stay inside these ranges and needn't reach their ends.
Inputs may be any that keep to these rules, and one draw needn't show every extreme that they name: `points`: point p of the leaf at grid position (x, y, z) lies in the unit cube [x, x + 1) x [y, y + 1) x [z, z + 1). `near_list`: slot s = 9 (dz + 1) + 3 (dy + 1) + (dx + 1), with dx, dy, dz in -1, 0, 1, names the leaf at grid offset (dx, dy, dz) from the row's leaf, or is -1; it is -1 wherever that position lies outside the grid; slot 13 names the leaf itself. `list_one`: in each row the named nodes come first and the -1 entries last, at least 6 named; each named node has the same index // 64 as the row's node.
All inputs are finite; a program needn't handle non-finite values.
Results may differ from the reference program's by a relative error of at most 0.0053.
Values may be sent and summed in bfloat16 or wider, within the bound.
A program may use at most 128 MiB of HBM per device.

```python
import jax
import jax.numpy as jnp
from jax import lax

PTS = 64
RANK = 32
RHS = 64
BX = 4
BY = 4
NEAR = 27
COUP1 = 12
TOPC = 16
LEAF_DEV = 64
GX = 32
GY = 128
GZ = 4
LEAVES = 16384
POINTS = 1048576
NODES1 = 2048
NODES2 = 256
BLOCK1 = 64


def leaf_place(index):
    column_count = GX // BX
    device = index // LEAF_DEV
    local = index % LEAF_DEV
    row_block = device // column_count
    col_block = device % column_count
    upper = local // 64
    lower = local % 64
    xpos = col_block * BX + lower // 8 % 2 * 2 + lower % 2
    ypos = row_block * BY + lower // 16 % 2 * 2 + lower // 2 % 2
    zpos = upper * 4 + lower // 32 % 2 * 2 + lower // 4 % 2
    return (xpos, ypos, zpos)


def leaf_number(xpos, ypos, zpos):
    column_count = GX // BX
    col_block = xpos // BX
    row_block = ypos // BY
    local_x = xpos % BX
    local_y = ypos % BY
    upper = zpos // 4
    local_z = zpos % 4
    lower = local_x % 2 + 2 * (local_y % 2) + 4 * (local_z % 2) + 8 * (local_x // 2) + 16 * (local_y // 2) + 32 * (local_z // 2)
    return (row_block * column_count + col_block) * LEAF_DEV + upper * 64 + lower


def draw_points(key, part):
    inner_key = jax.random.fold_in(key, 31)
    pick_key = jax.random.fold_in(key, 32)
    close_key = jax.random.fold_in(key, 33)
    leaf_index = jnp.arange(POINTS, dtype=jnp.int32) // PTS
    xpos, ypos, zpos = leaf_place(leaf_index)
    corner = jnp.stack([xpos, ypos, zpos]).astype(jnp.float32)
    spread_inside = jax.random.uniform(inner_key, (3, POINTS), jnp.float32, 0.0, 0.999)
    close_offset = 0.03 * jax.random.uniform(close_key, (3, POINTS), jnp.float32, 0.0, 1.0)
    picked = jax.random.randint(pick_key, (3, POINTS), 0, 4, dtype=jnp.int32)
    inside = jnp.where(picked == 0, close_offset, jnp.where(picked == 1, 0.999 - close_offset, spread_inside))
    return corner + inside


def draw_near_list(key, part):
    drop_key = jax.random.fold_in(key, 41)
    leaf_index = jnp.arange(LEAVES, dtype=jnp.int32)[:, None]
    slot = jnp.arange(27, dtype=jnp.int32)[None, :]
    step_x = slot % 3 - 1
    step_y = slot // 3 % 3 - 1
    step_z = slot // 9 - 1
    xpos, ypos, zpos = leaf_place(leaf_index)
    near_x = xpos + step_x
    near_y = ypos + step_y
    near_z = zpos + step_z
    inside = (near_x >= 0) & (near_x < GX) & (near_y >= 0) & (near_y < GY) & (near_z >= 0) & (near_z < GZ)
    keep = jax.random.randint(drop_key, (LEAVES, 27), 0, 4, dtype=jnp.int32) > 0
    keep = keep | (slot == 13)
    target = leaf_number(jnp.clip(near_x, 0, GX - 1), jnp.clip(near_y, 0, GY - 1), jnp.clip(near_z, 0, GZ - 1))
    return jnp.where(inside & keep, target, -1).astype(jnp.int32)


def draw_list_one(key, part):
    first_key = jax.random.fold_in(key, 21)
    second_key = jax.random.fold_in(key, 22)
    node_index = jnp.arange(NODES1, dtype=jnp.int32)[:, None]
    group_start = node_index // BLOCK1 * BLOCK1
    partner = group_start + jax.random.randint(first_key, (NODES1, COUP1), 0, BLOCK1, dtype=jnp.int32)
    filled = jax.random.randint(second_key, (NODES1, 1), COUP1 // 2, COUP1 + 1, dtype=jnp.int32)
    slot_index = jnp.arange(COUP1, dtype=jnp.int32)[None, :]
    return jnp.where(slot_index < filled, partner, -1).astype(jnp.int32)


def set_ends(result, key, low, largest):
    longest = result.shape.index(max(result.shape))
    spots = []
    for shift in (0, 1):
        where = [jax.random.randint(jax.random.fold_in(key, axis), (), 0, length) for axis, length in enumerate(result.shape)]
        where[longest] = (where[longest] + shift) % result.shape[longest]
        spots.append(tuple(where))
    return result.at[spots[0]].set(low).at[spots[1]].set(largest)


def block_levels(rng, extent, split, low, top_value):
    level, own = 1.0, jax.random.fold_in(rng, 6)
    for axis_at, shards_of in split:
        steps = jnp.exp(jax.random.uniform(jax.random.fold_in(own, axis_at), (shards_of,), jnp.float32, low / len(split), top_value / len(split)))
        level = level * jnp.repeat(steps, extent[axis_at] // shards_of).reshape([-1 if axis == axis_at else 1 for axis in range(len(extent))])
    return level


def gaussian(key, dims, width, most, split=(), kind=jnp.bfloat16):
    result = jax.random.normal(key, dims, jnp.float32) * width
    if len(split) > 0:
        result = block_levels(key, dims, split, -0.22, 0.18) * result
    return jnp.clip(result, min=-most, max=most).astype(kind)


def setup_inputs(seed: int = 0) -> dict:
    streams_of = jax.random.split(jax.random.key(seed), 11)
    charges = gaussian(streams_of[0], (RHS, POINTS), 1.0, 6.0, ((1, 256),))
    points = draw_points(jax.random.fold_in(streams_of[10], 71), 0)
    leaf_basis = gaussian(streams_of[2], (RANK, POINTS), PTS ** -0.5, 0.75, ((1, 256),))
    transfer_one = gaussian(streams_of[3], (LEAVES, RANK, RANK), (4 * RANK) ** -0.5, 0.5, ((0, 256),))
    transfer_two = gaussian(streams_of[4], (NODES1, RANK, RANK), (4 * RANK) ** -0.5, 0.5, ((0, 256),))
    couple_one = gaussian(streams_of[5], (NODES1, COUP1, RANK, RANK), (COUP1 * RANK) ** -0.5, 0.3125, ((0, 256),))
    couple_two = gaussian(streams_of[6], (NODES2, TOPC, RANK, RANK), (TOPC * RANK) ** -0.5, 0.25, ((0, 256),))
    near_list = draw_near_list(jax.random.fold_in(streams_of[10], 71), 0)
    list_one = draw_list_one(jax.random.fold_in(streams_of[10], 71), 0)
    list_two = set_ends(jax.random.randint(streams_of[9], (NODES2, TOPC), 0, NODES2), jax.random.fold_in(streams_of[9], 1), 0, NODES2 - 1).astype(jnp.int32)
    return {"charges": charges, "points": points, "leaf_basis": leaf_basis, "transfer_one": transfer_one, "transfer_two": transfer_two, "couple_one": couple_one, "couple_two": couple_two, "near_list": near_list, "list_one": list_one, "list_two": list_two}


softening = 0.0025

def leaf_block(source, remote, values, active):
    distance = source[:, None, :, :, None] - remote[:, :, :, None, :]
    kernel = (active[:, :, None, None] / jnp.sqrt(lax.optimization_barrier(jnp.sum(distance * distance, axis=2)) + softening)).astype(jnp.bfloat16)
    return jnp.einsum('lsij,lsrj->lri', kernel.astype(jnp.float32), values.astype(jnp.float32))

def reference(charges, points, leaf_basis, transfer_one, transfer_two, couple_one, couple_two, near_list, list_one, list_two):
    charge_leaf = charges.reshape(RHS, LEAVES, PTS).transpose(1, 0, 2)
    point_leaf = points.reshape(3, LEAVES, PTS).transpose(1, 0, 2)
    basis_leaf = leaf_basis.reshape(RANK, LEAVES, PTS).astype(jnp.float32)

    def near_step(block_index):
        offset = block_index * 64
        leaf_ids = lax.dynamic_slice_in_dim(near_list, offset, 64, 0)
        active = (leaf_ids >= 0).astype(jnp.float32)
        safe_ids = jnp.maximum(leaf_ids, 0)
        source = lax.dynamic_slice_in_dim(point_leaf, offset, 64, 0)
        return leaf_block(source, point_leaf[safe_ids], charge_leaf[safe_ids], active)
    near_part = lax.map(near_step, jnp.arange(LEAVES // 64, dtype=jnp.int32)).reshape(LEAVES, RHS, PTS)
    coef_leaf = jnp.einsum('kln,lrn->lkr', basis_leaf, charge_leaf.astype(jnp.float32)).astype(jnp.bfloat16)
    lifted = jnp.einsum('lab,lar->lbr', transfer_one.astype(jnp.float32), coef_leaf.astype(jnp.float32))
    coef_one = lifted.reshape(NODES1, 8, RANK, RHS).sum(axis=1).astype(jnp.bfloat16)
    lifted_two = jnp.einsum('lab,lar->lbr', transfer_two.astype(jnp.float32), coef_one.astype(jnp.float32))
    coef_two = lifted_two.reshape(NODES2, 8, RANK, RHS).sum(axis=1).astype(jnp.bfloat16)

    def couple_step(block_index):
        offset = block_index * 64
        partner_ids = lax.dynamic_slice_in_dim(list_one, offset, 64, 0)
        matrices = lax.dynamic_slice_in_dim(couple_one, offset, 64, 0)
        active = (partner_ids >= 0).astype(jnp.bfloat16)
        partner = coef_one[jnp.maximum(partner_ids, 0)] * active[:, :, None, None]
        return jnp.einsum('psab,psbr->par', matrices.astype(jnp.float32), partner.astype(jnp.float32))
    field_one = lax.map(couple_step, jnp.arange(NODES1 // 64, dtype=jnp.int32)).reshape(NODES1, RANK, RHS)
    field_two = jnp.einsum('psab,psbr->par', couple_two.astype(jnp.float32), coef_two[list_two].astype(jnp.float32))
    down_one = field_one + jnp.einsum('pab,pbr->par', transfer_two.astype(jnp.float32), jnp.repeat(field_two, 8, axis=0), precision=lax.Precision.HIGHEST)
    down_leaf = jnp.einsum('lab,lbr->lar', transfer_one.astype(jnp.float32), jnp.repeat(down_one, 8, axis=0), precision=lax.Precision.HIGHEST).astype(jnp.bfloat16)
    far_part = jnp.einsum('kln,lkr->lrn', basis_leaf, down_leaf.astype(jnp.float32))
    potential = near_part * (NEAR * PTS) ** (-0.5) + far_part
    return potential.transpose(1, 0, 2).reshape(RHS, LEAVES * PTS).astype(jnp.bfloat16)
```

```python
import jax
import jax.numpy as jnp
import numpy as np
from jax import lax
from jax.experimental import pallas as pl
from jax.experimental.pallas import tpu as pltpu
from jax.sharding import PartitionSpec as P

F32 = jnp.float32
BF16 = jnp.bfloat16
MESH = pl.DeviceIdType.MESH
NT = (((1,), (1,)), ((), ()))
TN = (((0,), (0,)), ((), ()))
NN = (((1,), (0,)), ((), ()))

ROWS = 32
COLS = 8
SOFT = 0.0025
SCALE = (27 * 64) ** (-0.5)


def mm(a, b, dims=NN):
    return lax.dot_general(a, b, dims, preferred_element_type=F32)


def picks():
    pick = np.zeros((256, 192), np.float32)
    sides = (((0, 1, 1, 2, 3), (0, -1, 1, 0, -1)), ((0, 1, 2, 2, 3), (1, 0, -1, 1, 0)))
    for side, (places, steps) in enumerate(sides):
        for x in range(4):
            for y in range(4):
                for tile in range(5):
                    z = places[tile]
                    leaf = x % 2 + 2 * (y % 2) + 4 * (z % 2) + 8 * (x // 2) + 16 * (y // 2) + 32 * (z // 2)
                    pick[side * 128 + (x * 4 + y) * 8 + tile, (steps[tile] + 1) * 64 + leaf] = 1
    return pick


def body(
    charges,
    points,
    basis,
    t_one,
    t_two,
    c_one,
    c_two,
    near_list,
    list_one,
    list_two,
    pick,
    out,
    ext_c,
    ext_p,
    wide_c,
    src_f,
    own_f,
    masks,
    shifted,
    near,
    split_basis,
    coef,
    one_send,
    one_all,
    two_send,
    two_all,
    ctwo_send,
    ctwo_all,
    lists_send,
    lists_all,
    lists_s,
    chosen,
    field,
    part_send,
    part_all,
    halo_s,
    halo_r,
    one_s,
    one_r,
    two_s,
    two_r,
    ctwo_s,
    ctwo_r,
    lt_s,
    lt_r,
    part_s,
    part_r,
    local,
):
    r = lax.axis_index("row")
    c = lax.axis_index("col")
    barrier = pltpu.get_barrier_semaphore()

    def greet_col(k, _):
        pl.semaphore_signal(barrier, inc=1, device_id=(r, lax.rem(c + k, COLS)), device_id_type=MESH)
        return 0

    def greet_row(k, _):
        pl.semaphore_signal(barrier, inc=1, device_id=(lax.rem(r + k, ROWS), c), device_id_type=MESH)
        return 0

    lax.fori_loop(1, COLS, greet_col, 0)
    lax.fori_loop(1, ROWS, greet_row, 0)

    low = lax.broadcasted_iota(jnp.int32, (64, 128), 1) < 64

    def halves(a, b, upper):
        if upper:
            return jnp.concatenate([a[:, 64:], b[:, 64:]], axis=1)
        return jnp.concatenate([a[:, :64], b[:, :64]], axis=1)

    def arrange(i, _):
        x1, y = i // 4, lax.rem(i, 4)
        for h in range(2):
            tile = lax.rem(y, 2) + 4 * x1 + 8 * (y // 2) + 16 * h
            first = pl.ds(pl.multiple_of(tile * 128, 128), 128)
            second = pl.ds(pl.multiple_of(tile * 128 + 256, 128), 128)
            at = slice(h * 128, h * 128 + 128)
            a, b = charges[:, first], charges[:, second]
            pa, pb = points[:, first], points[:, second]
            for x0 in range(2):
                ext_c[1 + y, 1 + 2 * x1 + x0, :, at] = halves(a, b, x0)
                ext_p[1 + y, 1 + 2 * x1 + x0, 0:3, at] = halves(pa, pb, x0)
                ext_p[1 + y, 1 + 2 * x1 + x0, 3:4, at] = jnp.zeros((1, 128), F32)
        return 0

    lax.fori_loop(0, 8, arrange, 0)

    ctwo_send[...] = jnp.concatenate([c_two[s] for s in range(16)], axis=1)
    lists_send[...] = jnp.zeros_like(lists_send)
    lists_send[0:1, 0:16] = list_two[...]

    pl.semaphore_wait(barrier, COLS + ROWS - 2)

    def halo(n, ref, src, dst, device):
        return pltpu.make_async_remote_copy(
            src_ref=ref.at[src],
            dst_ref=ref.at[dst],
            send_sem=halo_s.at[n],
            recv_sem=halo_r.at[n],
            device_id=device,
            device_id_type=MESH,
        )

    right, left = (r, lax.rem(c + 1, COLS)), (r, lax.rem(c + COLS - 1, COLS))
    up, down = (lax.rem(r + 1, ROWS), c), (lax.rem(r + ROWS - 1, ROWS), c)
    four = pl.ds(1, 4)
    x_halo, y_halo, corners = [], [], []
    for i, ref in enumerate((ext_c, ext_p)):
        x_halo.append(halo(8 * i + 0, ref, (four, 4), (four, 0), right))
        x_halo.append(halo(8 * i + 1, ref, (four, 1), (four, 5), left))
        y_halo.append(halo(8 * i + 2, ref, (4, four), (0, four), up))
        y_halo.append(halo(8 * i + 3, ref, (1, four), (5, four), down))
        corners.append(halo(8 * i + 4, ref, (4, 0), (0, 0), up))
        corners.append(halo(8 * i + 5, ref, (4, 5), (0, 5), up))
        corners.append(halo(8 * i + 6, ref, (1, 0), (5, 0), down))
        corners.append(halo(8 * i + 7, ref, (1, 5), (5, 5), down))
    for copy in x_halo + y_halo:
        copy.start()

    def to_col(k, src, ref, send, recv):
        return pltpu.make_async_remote_copy(
            src_ref=src,
            dst_ref=ref.at[c],
            send_sem=send.at[k],
            recv_sem=recv.at[k],
            device_id=(r, lax.rem(c + k, COLS)),
            device_id_type=MESH,
        )

    def to_row(k):
        return pltpu.make_async_remote_copy(
            src_ref=two_send,
            dst_ref=two_all.at[r],
            send_sem=two_s.at[k],
            recv_sem=two_r.at[k],
            device_id=(lax.rem(r + k, ROWS), c),
            device_id_type=MESH,
        )

    def couple_copies(k):
        return to_col(k, ctwo_send, ctwo_all, ctwo_s, ctwo_r), to_col(k, lists_send, lists_all, lt_s, lt_r)

    def start_couple(k, _):
        for copy in couple_copies(k):
            copy.start()
        return 0

    lax.fori_loop(1, COLS, start_couple, 0)
    ctwo_all[c] = ctwo_send[...]
    lists_all[c] = lists_send[...]

    for tile in range(32):
        b = basis[:, tile * 128 : tile * 128 + 128]
        zero = jnp.zeros((32, 64), BF16)
        split_basis[tile] = jnp.concatenate(
            [jnp.concatenate([b[:, :64], zero], axis=1), jnp.concatenate([zero, b[:, 64:]], axis=1)], axis=0
        )

    def lift(n, _):
        for i in range(4):
            lanes = pl.ds(pl.multiple_of(n * 512 + i * 128, 128), 128)
            coef[n, i * 64 : i * 64 + 64] = mm(split_basis[n * 4 + i], charges[:, lanes], NT).astype(BF16)
        field[n] = mm(t_one[n], coef[n], TN)
        return 0

    lax.fori_loop(0, 8, lift, 0)
    ones = [field[n].astype(BF16) for n in range(8)]
    for i in range(4):
        one_send[i] = jnp.concatenate([ones[2 * i], ones[2 * i + 1]], axis=1)
    two = mm(t_two[...], jnp.concatenate(ones, axis=0), TN).astype(BF16)
    two_send[...] = jnp.concatenate([two[:16], two[16:]], axis=1)

    def start_two(k, _):
        to_row(k).start()
        return 0

    def start_one(k, _):
        to_col(k, one_send, one_all, one_s, one_r).start()
        return 0

    lax.fori_loop(1, ROWS, start_two, 0)
    lax.fori_loop(1, COLS, start_one, 0)
    one_all[c] = one_send[...]
    one_all[COLS] = jnp.zeros((4, 32, 128), BF16)
    two_all[r] = two_send[...]
    two_all[ROWS] = jnp.zeros((16, 128), BF16)

    active = jnp.where(near_list[...] >= 0, 1.0, 0.0)
    lists = jnp.concatenate([active[:, 0:9], active[:, 9:18], active[:, 18:27]], axis=0).astype(BF16)
    blocked = jnp.where(mm(pick[...], lists) > 0.5, 0.0, jnp.inf)
    low2 = lax.broadcasted_iota(jnp.int32, (128, 128), 1) < 64
    for j in range(9):
        masks[j] = jnp.where(low2, blocked[0:128, j : j + 1], blocked[128:256, j : j + 1])

    coord = lax.broadcasted_iota(jnp.int32, (4, 256), 0)
    middle = jnp.where(coord == 0, 4 * c + 2, jnp.where(coord == 1, 4 * r + 2, jnp.where(coord == 2, 2, 0))).astype(F32)

    def prepare(y, x):
        p = ext_p[y, x] - middle
        q = p * p
        size = q[0:1] + q[1:2] + q[2:3]
        f = jnp.concatenate([-2.0 * p[0:3], size, jnp.zeros((4, 256), F32)], axis=0)
        e = y * 6 + x
        f0, f1 = f[:, :128], f[:, 128:]
        src_f[e, 0:8] = f0
        src_f[e, 8:16] = jnp.where(low[:8], f1, f0)
        src_f[e, 16:24] = f1
        ch = ext_c[y, x]
        c0, c1 = ch[:, :128], ch[:, 128:]
        zero = jnp.zeros((64, 64), BF16)
        wide_c[e, :, 0:128] = c0
        wide_c[e, :, 128:256] = jnp.concatenate([c1[:, :64], zero], axis=1)
        wide_c[e, :, 256:384] = c1
        wide_c[e, :, 384:512] = jnp.concatenate([zero, c0[:, 64:]], axis=1)
        return p, size

    def own_column(i, _):
        x, y = i // 4, lax.rem(i, 4)
        p, size = prepare(1 + y, 1 + x)
        features = (p[0:1], p[1:2], p[2:3], size + SOFT)
        for f, row in enumerate(features):
            for h in range(2):
                half = jnp.broadcast_to(row[:, h * 128 : h * 128 + 128], (128, 128))
                own_f[i, f, h * 128 : h * 128 + 128] = jnp.transpose(half)
            own_f[i, f, 256:320] = jnp.where(low, own_f[i, f, 64:128], own_f[i, f, 128:192])
        return 0

    lax.fori_loop(0, 16, own_column, 0)

    def unit(i):
        g, k = i // 4, lax.rem(i, 4)
        gx, gy, a, b = g // 2, lax.rem(g, 2), k // 2, lax.rem(k, 2)
        x = (1 - gx) * (1 + a) + gx * 3 * a
        y = (1 - gy) * (1 + b) + gy * 3 * b
        d = x * 4 + y
        total = [jnp.zeros((128, 64), F32), jnp.zeros((128, 64), F32)]
        zero = jnp.zeros((64, 128), BF16)
        for j in range(9):
            e = (y + j // 3) * 6 + x + j % 3
            rows = pl.ds(pl.multiple_of(d * 8, 8), 8)
            s0, sm, s1 = src_f[e, 0:8], src_f[e, 8:16], src_f[e, 16:24]
            m = masks[j, rows]

            def tile(t, first, s):
                dist = own_f[d, 3, first : first + 64] + (s[3:4] + m[t : t + 1])
                for f in range(3):
                    dist = dist + own_f[d, f, first : first + 64] * s[f : f + 1]
                return lax.rsqrt(dist.astype(BF16))

            mid = tile(2, 256, sm)
            k0 = jnp.concatenate(
                [jnp.concatenate([tile(0, 0, s0), zero], 1), jnp.concatenate([tile(1, 64, s0), mid], 1)], 0
            )
            k1 = jnp.concatenate(
                [jnp.concatenate([tile(3, 128, s1), mid], 1), jnp.concatenate([tile(4, 192, s1), zero], 1)], 0
            )
            total[0] = total[0] + mm(k0, wide_c[e, :, 0:256], NT)
            total[1] = total[1] + mm(k1, wide_c[e, :, 256:512], NT)
        near[d, :, 0:128] = jnp.transpose(total[0])
        near[d, :, 128:256] = jnp.transpose(total[1])

    def unit_step(i, _):
        unit(i)
        return 0

    lax.fori_loop(0, 4, unit_step, 0)

    for copy in x_halo:
        copy.wait()
    for copy in corners:
        copy.start()

    def wait_couple(k, _):
        for copy in couple_copies(k):
            copy.wait()
        return 0

    def wait_two(k, _):
        to_row(k).wait()
        return 0

    def wait_one(k, _):
        to_col(k, one_send, one_all, one_s, one_r).wait()
        return 0

    lax.fori_loop(1, COLS, wait_couple, 0)
    to_scalar = pltpu.make_async_copy(lists_all, lists_s, local)
    to_scalar.start()
    to_scalar.wait()
    lax.fori_loop(1, ROWS, wait_two, 0)

    def share(k, _):
        peer = lax.rem(c + k, COLS)
        for s in range(16):
            node = lists_s[peer, 0, s]
            at = jnp.where(lax.rem(node, COLS) == c, node // COLS, ROWS)
            v = two_all[at]
            chosen[s * 32 : s * 32 + 16] = v[:, :64]
            chosen[s * 32 + 16 : s * 32 + 32] = v[:, 64:]
        part = mm(ctwo_all[peer], chosen[...])
        part_send[k] = jnp.concatenate([part[:16], part[16:]], axis=1)
        return 0

    def part_copy(k):
        return to_col(k, part_send.at[k], part_all, part_s, part_r)

    def share_and_send(k, _):
        share(k, 0)
        part_copy(k).start()
        return 0

    lax.fori_loop(1, COLS, share_and_send, 0)
    share(0, 0)
    part_all[c] = part_send[0]

    lax.fori_loop(1, COLS, wait_one, 0)
    start = r * 64

    def couple(n, _):
        for s in range(12):
            node = list_one[n, s]
            p = jnp.clip(node - start, 0, 63)
            at = jnp.where(node >= 0, p // 8, COLS)
            v = one_all[at, lax.rem(p, 8) // 2]
            chosen[s * 32 : s * 32 + 32] = jnp.where(lax.rem(p, 2) == 1, v[:, 64:], v[:, :64])
        wide = jnp.concatenate([c_one[n, s] for s in range(12)], axis=1)
        field[n] = mm(wide, chosen[0:384])
        return 0

    lax.fori_loop(0, 8, couple, 0)

    for copy in y_halo:
        copy.wait()

    def beside(i, _):
        prepare(0, 1 + i)
        prepare(5, 1 + i)
        prepare(1 + i, 0)
        prepare(1 + i, 5)
        return 0

    lax.fori_loop(0, 4, beside, 0)
    lax.fori_loop(4, 12, unit_step, 0)
    for copy in corners:
        copy.wait()
    for y in (0, 5):
        for x in (0, 5):
            prepare(y, x)
    lax.fori_loop(12, 16, unit_step, 0)

    def wait_part(k, _):
        part_copy(k).wait()
        return 0

    lax.fori_loop(1, COLS, wait_part, 0)
    part = part_all[0]
    for k in range(1, COLS):
        part = part + part_all[k]
    top = jnp.concatenate([part[:, :64], part[:, 64:]], axis=0)
    top_high = top.astype(BF16)
    top_low = (top - top_high.astype(F32)).astype(BF16)

    def lower(n, _):
        rows = pl.ds(pl.multiple_of(n * 32, 32), 32)
        t = t_two[rows]
        one = field[n] + mm(t, top_high) + mm(t, top_low)
        high = one.astype(BF16)
        rest = (one - high.astype(F32)).astype(BF16)
        coef[n] = (mm(t_one[n], high) + mm(t_one[n], rest)).astype(BF16)
        return 0

    lax.fori_loop(0, 8, lower, 0)

    def finish(i, _):
        x1, y = i // 4, lax.rem(i, 4)
        even, odd = 2 * x1 * 4 + y, (2 * x1 + 1) * 4 + y
        for h in range(2):
            at = slice(h * 128, h * 128 + 128)
            a, b = near[even, :, at], near[odd, :, at]
            for z0 in range(2):
                tile = lax.rem(y, 2) + 2 * z0 + 4 * x1 + 8 * (y // 2) + 16 * h
                rows = pl.ds(pl.multiple_of(lax.rem(tile, 4) * 64, 64), 64)
                far = mm(coef[tile // 4, rows], split_basis[tile], TN)
                lanes = pl.ds(pl.multiple_of(tile * 128, 128), 128)
                out[:, lanes] = (halves(a, b, z0) * SCALE + far).astype(BF16)
        return 0

    lax.fori_loop(0, 8, finish, 0)


def shards(charges, points, leaf_basis, transfer_one, transfer_two, couple_one, couple_two, near_list, list_one, list_two):
    vmem = pl.BlockSpec(memory_space=pltpu.VMEM)
    smem = pl.BlockSpec(memory_space=pltpu.SMEM)
    dma = pltpu.SemaphoreType.DMA
    return pl.pallas_call(
        body,
        out_shape=jax.ShapeDtypeStruct(charges.shape, BF16),
        in_specs=[vmem] * 8 + [smem, vmem, vmem],
        out_specs=vmem,
        scratch_shapes=[
            pltpu.VMEM((6, 6, 64, 256), BF16),
            pltpu.VMEM((6, 6, 4, 256), F32),
            pltpu.VMEM((36, 64, 512), BF16),
            pltpu.VMEM((36, 24, 128), F32),
            pltpu.VMEM((16, 4, 320, 128), F32),
            pltpu.VMEM((9, 128, 128), F32),
            pltpu.VMEM((8, 128), F32),
            pltpu.VMEM((16, 64, 256), F32),
            pltpu.VMEM((32, 64, 128), BF16),
            pltpu.VMEM((8, 256, 64), BF16),
            pltpu.VMEM((4, 32, 128), BF16),
            pltpu.VMEM((9, 4, 32, 128), BF16),
            pltpu.VMEM((16, 128), BF16),
            pltpu.VMEM((33, 16, 128), BF16),
            pltpu.VMEM((32, 512), BF16),
            pltpu.VMEM((8, 32, 512), BF16),
            pltpu.VMEM((8, 128), jnp.int32),
            pltpu.VMEM((8, 8, 128), jnp.int32),
            pltpu.SMEM((8, 8, 128), jnp.int32),
            pltpu.VMEM((512, 64), BF16),
            pltpu.VMEM((8, 32, 64), F32),
            pltpu.VMEM((8, 16, 128), F32),
            pltpu.VMEM((8, 16, 128), F32),
            dma((16,)),
            dma((16,)),
            dma((COLS,)),
            dma((COLS,)),
            dma((ROWS,)),
            dma((ROWS,)),
            dma((COLS,)),
            dma((COLS,)),
            dma((COLS,)),
            dma((COLS,)),
            dma((COLS,)),
            dma((COLS,)),
            dma,
        ],
        compiler_params=pltpu.CompilerParams(
            collective_id=0, has_side_effects=True, vmem_limit_bytes=58 * 2**20
        ),
    )(
        charges,
        points,
        leaf_basis,
        transfer_one.reshape(8, 256, 32),
        transfer_two.reshape(256, 32),
        couple_one,
        couple_two.reshape(16, 32, 32),
        near_list,
        list_one,
        list_two,
        jnp.asarray(picks(), BF16),
    )


def solution(mesh):
    lead = ("row", "col")
    columns, three = P(None, lead), P(lead, None, None)
    four, two = P(lead, None, None, None), P(lead, None)
    in_specs = (columns, columns, columns, three, three, four, four, two, two, two)
    return jax.shard_map(shards, mesh=mesh, in_specs=in_specs, out_specs=columns, check_vma=False)
```

```python
import jax
import jax.numpy as jnp
import numpy as np
from jax import lax
from jax.experimental import pallas as pl
from jax.experimental.pallas import tpu as pltpu
from jax.sharding import PartitionSpec as P

F32 = jnp.float32
BF16 = jnp.bfloat16
MESH = pl.DeviceIdType.MESH
NT = (((1,), (1,)), ((), ()))
TN = (((0,), (0,)), ((), ()))
NN = (((1,), (0,)), ((), ()))

ROWS = 32
COLS = 8
SOFT = 0.0025
SCALE = (27 * 64) ** (-0.5)


def mm(a, b, dims=NN):
    return lax.dot_general(a, b, dims, preferred_element_type=F32)


def picks():
    pick = np.zeros((256, 192), np.float32)
    sides = (((0, 1, 1, 2, 3), (0, -1, 1, 0, -1)), ((0, 1, 2, 2, 3), (1, 0, -1, 1, 0)))
    for side, (places, steps) in enumerate(sides):
        for x in range(4):
            for y in range(4):
                for tile in range(5):
                    z = places[tile]
                    leaf = x % 2 + 2 * (y % 2) + 4 * (z % 2) + 8 * (x // 2) + 16 * (y // 2) + 32 * (z // 2)
                    pick[side * 128 + (x * 4 + y) * 8 + tile, (steps[tile] + 1) * 64 + leaf] = 1
    return pick


def body(
    charges,
    points,
    basis,
    t_one,
    t_two,
    c_one,
    c_two,
    near_list,
    list_one,
    list_two,
    pick,
    out,
    ext_c,
    ext_p,
    wide_c,
    src_f,
    own_f,
    masks,
    shifted,
    near,
    split_basis,
    coef,
    one_send,
    one_all,
    two_send,
    two_all,
    ctwo_send,
    ctwo_all,
    lists_send,
    lists_all,
    lists_s,
    chosen,
    field,
    part_send,
    part_all,
    halo_s,
    halo_r,
    one_s,
    one_r,
    two_s,
    two_r,
    ctwo_s,
    ctwo_r,
    lt_s,
    lt_r,
    part_s,
    part_r,
    local,
):
    r = lax.axis_index("row")
    c = lax.axis_index("col")
    barrier = pltpu.get_barrier_semaphore()

    def greet_col(k, _):
        pl.semaphore_signal(barrier, inc=1, device_id=(r, lax.rem(c + k, COLS)), device_id_type=MESH)
        return 0

    def greet_row(k, _):
        pl.semaphore_signal(barrier, inc=1, device_id=(lax.rem(r + k, ROWS), c), device_id_type=MESH)
        return 0

    lax.fori_loop(1, COLS, greet_col, 0)
    lax.fori_loop(1, ROWS, greet_row, 0)

    low = lax.broadcasted_iota(jnp.int32, (64, 128), 1) < 64

    def halves(a, b, upper):
        if upper:
            return jnp.concatenate([a[:, 64:], b[:, 64:]], axis=1)
        return jnp.concatenate([a[:, :64], b[:, :64]], axis=1)

    def arrange(i, _):
        x1, y = i // 4, lax.rem(i, 4)
        for h in range(2):
            tile = lax.rem(y, 2) + 4 * x1 + 8 * (y // 2) + 16 * h
            first = pl.ds(pl.multiple_of(tile * 128, 128), 128)
            second = pl.ds(pl.multiple_of(tile * 128 + 256, 128), 128)
            at = slice(h * 128, h * 128 + 128)
            a, b = charges[:, first], charges[:, second]
            pa, pb = points[:, first], points[:, second]
            for x0 in range(2):
                ext_c[1 + y, 1 + 2 * x1 + x0, :, at] = halves(a, b, x0)
                ext_p[1 + y, 1 + 2 * x1 + x0, 0:3, at] = halves(pa, pb, x0)
                ext_p[1 + y, 1 + 2 * x1 + x0, 3:4, at] = jnp.zeros((1, 128), F32)
        return 0

    lax.fori_loop(0, 8, arrange, 0, unroll=True)

    ctwo_send[...] = jnp.concatenate([c_two[s] for s in range(16)], axis=1)
    lists_send[...] = jnp.zeros_like(lists_send)
    lists_send[0:1, 0:16] = list_two[...]

    pl.semaphore_wait(barrier, COLS + ROWS - 2)

    def halo(n, ref, src, dst, device):
        return pltpu.make_async_remote_copy(
            src_ref=ref.at[src],
            dst_ref=ref.at[dst],
            send_sem=halo_s.at[n],
            recv_sem=halo_r.at[n],
            device_id=device,
            device_id_type=MESH,
        )

    right, left = (r, lax.rem(c + 1, COLS)), (r, lax.rem(c + COLS - 1, COLS))
    up, down = (lax.rem(r + 1, ROWS), c), (lax.rem(r + ROWS - 1, ROWS), c)
    four = pl.ds(1, 4)
    x_halo, y_halo, corners = [], [], []
    for i, ref in enumerate((ext_c, ext_p)):
        x_halo.append(halo(8 * i + 0, ref, (four, 4), (four, 0), right))
        x_halo.append(halo(8 * i + 1, ref, (four, 1), (four, 5), left))
        y_halo.append(halo(8 * i + 2, ref, (4, four), (0, four), up))
        y_halo.append(halo(8 * i + 3, ref, (1, four), (5, four), down))
        corners.append(halo(8 * i + 4, ref, (4, 0), (0, 0), up))
        corners.append(halo(8 * i + 5, ref, (4, 5), (0, 5), up))
        corners.append(halo(8 * i + 6, ref, (1, 0), (5, 0), down))
        corners.append(halo(8 * i + 7, ref, (1, 5), (5, 5), down))
    for copy in y_halo:
        copy.start()

    def to_col(k, src, ref, send, recv):
        return pltpu.make_async_remote_copy(
            src_ref=src,
            dst_ref=ref.at[c],
            send_sem=send.at[k],
            recv_sem=recv.at[k],
            device_id=(r, lax.rem(c + k, COLS)),
            device_id_type=MESH,
        )

    def to_row(k):
        return pltpu.make_async_remote_copy(
            src_ref=two_send,
            dst_ref=two_all.at[r],
            send_sem=two_s.at[k],
            recv_sem=two_r.at[k],
            device_id=(lax.rem(r + k, ROWS), c),
            device_id_type=MESH,
        )

    def couple_copies(k):
        return to_col(k, ctwo_send, ctwo_all, ctwo_s, ctwo_r), to_col(k, lists_send, lists_all, lt_s, lt_r)

    def start_couple(k, _):
        for copy in couple_copies(k):
            copy.start()
        return 0

    lax.fori_loop(1, COLS, start_couple, 0)
    for copy in x_halo:
        copy.start()
    ctwo_all[c] = ctwo_send[...]
    lists_all[c] = lists_send[...]

    for tile in range(32):
        b = basis[:, tile * 128 : tile * 128 + 128]
        zero = jnp.zeros((32, 64), BF16)
        split_basis[tile] = jnp.concatenate(
            [jnp.concatenate([b[:, :64], zero], axis=1), jnp.concatenate([zero, b[:, 64:]], axis=1)], axis=0
        )

    def lift(n, _):
        for i in range(4):
            lanes = pl.ds(pl.multiple_of(n * 512 + i * 128, 128), 128)
            coef[n, i * 64 : i * 64 + 64] = mm(split_basis[n * 4 + i], charges[:, lanes], NT).astype(BF16)
        field[n] = mm(t_one[n], coef[n], TN)
        return 0

    lax.fori_loop(0, 8, lift, 0, unroll=True)
    ones = [field[n].astype(BF16) for n in range(8)]
    for i in range(4):
        one_send[i] = jnp.concatenate([ones[2 * i], ones[2 * i + 1]], axis=1)
    two = mm(t_two[...], jnp.concatenate(ones, axis=0), TN).astype(BF16)
    two_send[...] = jnp.concatenate([two[:16], two[16:]], axis=1)

    def start_two(k, _):
        to_row(k).start()
        return 0

    def start_one(k, _):
        to_col(k, one_send, one_all, one_s, one_r).start()
        return 0

    lax.fori_loop(1, ROWS, start_two, 0)
    lax.fori_loop(1, COLS, start_one, 0)
    one_all[c] = one_send[...]
    one_all[COLS] = jnp.zeros((4, 32, 128), BF16)
    two_all[r] = two_send[...]
    two_all[ROWS] = jnp.zeros((16, 128), BF16)

    active = jnp.transpose(jnp.where(near_list[...] >= 0, 1.0, 0.0))
    lists = jnp.concatenate([active[:, 0:9], active[:, 9:18], active[:, 18:27]], axis=0).astype(BF16)
    blocked = jnp.where(mm(pick[...], lists) > 0.5, 0.0, jnp.inf)
    low2 = lax.broadcasted_iota(jnp.int32, (128, 128), 1) < 64
    for j in range(9):
        masks[j] = jnp.where(low2, blocked[0:128, j : j + 1], blocked[128:256, j : j + 1])

    coord = lax.broadcasted_iota(jnp.int32, (4, 256), 0)
    middle = jnp.where(coord == 0, 4 * c + 2, jnp.where(coord == 1, 4 * r + 2, jnp.where(coord == 2, 2, 0))).astype(F32)

    def prepare(y, x):
        p = ext_p[y, x] - middle
        q = p * p
        size = q[0:1] + q[1:2] + q[2:3]
        f = jnp.concatenate([-2.0 * p[0:3], size, jnp.zeros((4, 256), F32)], axis=0)
        e = y * 6 + x
        f0, f1 = f[:, :128], f[:, 128:]
        src_f[e, 0:8] = f0
        src_f[e, 8:16] = jnp.where(low[:8], f1, f0)
        src_f[e, 16:24] = f1
        ch = ext_c[y, x]
        c0, c1 = ch[:, :128], ch[:, 128:]
        zero = jnp.zeros((64, 64), BF16)
        wide_c[e, :, 0:128] = c0
        wide_c[e, :, 128:256] = jnp.concatenate([c1[:, :64], zero], axis=1)
        wide_c[e, :, 256:384] = c1
        wide_c[e, :, 384:512] = jnp.concatenate([zero, c0[:, 64:]], axis=1)
        return p, size

    def own_column(i, _):
        x, y = i // 4, lax.rem(i, 4)
        p, size = prepare(1 + y, 1 + x)
        features = (p[0:1], p[1:2], p[2:3], size + SOFT)
        for f, row in enumerate(features):
            for h in range(2):
                half = jnp.broadcast_to(row[:, h * 128 : h * 128 + 128], (128, 128))
                own_f[i, f, h * 128 : h * 128 + 128] = jnp.transpose(half)
            own_f[i, f, 256:320] = jnp.where(low, own_f[i, f, 64:128], own_f[i, f, 128:192])
        return 0

    lax.fori_loop(0, 16, own_column, 0, unroll=2)

    def unit(i):
        g, k = i // 4, lax.rem(i, 4)
        gx, gy, a, b = g // 2, lax.rem(g, 2), k // 2, lax.rem(k, 2)
        x = (1 - gx) * (1 + a) + gx * 3 * a
        y = (1 - gy) * (1 + b) + gy * 3 * b
        d = x * 4 + y
        total = [jnp.zeros((128, 64), F32), jnp.zeros((128, 64), F32)]
        zero = jnp.zeros((64, 128), BF16)
        for j in range(9):
            e = (y + j // 3) * 6 + x + j % 3
            rows = pl.ds(pl.multiple_of(d * 8, 8), 8)
            s0, sm, s1 = src_f[e, 0:8], src_f[e, 8:16], src_f[e, 16:24]
            m = masks[j, rows]

            def tile(t, first, s):
                dist = own_f[d, 3, first : first + 64] + (s[3:4] + m[t : t + 1])
                for f in range(3):
                    dist = dist + own_f[d, f, first : first + 64] * s[f : f + 1]
                return lax.rsqrt(dist.astype(BF16))

            mid = tile(2, 256, sm)
            k0 = jnp.concatenate(
                [jnp.concatenate([tile(0, 0, s0), zero], 1), jnp.concatenate([tile(1, 64, s0), mid], 1)], 0
            )
            k1 = jnp.concatenate(
                [jnp.concatenate([tile(3, 128, s1), mid], 1), jnp.concatenate([tile(4, 192, s1), zero], 1)], 0
            )
            total[0] = total[0] + mm(k0, wide_c[e, :, 0:256], NT)
            total[1] = total[1] + mm(k1, wide_c[e, :, 256:512], NT)
        near[d, :, 0:128] = jnp.transpose(total[0])
        near[d, :, 128:256] = jnp.transpose(total[1])

    def unit_step(i, _):
        unit(i)
        return 0

    lax.fori_loop(0, 4, unit_step, 0)

    for copy in y_halo:
        copy.wait()

    def beside_y(i, _):
        prepare(0, 1 + i)
        prepare(5, 1 + i)
        return 0

    lax.fori_loop(0, 4, beside_y, 0, unroll=True)
    lax.fori_loop(4, 8, unit_step, 0)

    def wait_couple(k, _):
        for copy in couple_copies(k):
            copy.wait()
        return 0

    def wait_two(k, _):
        to_row(k).wait()
        return 0

    def wait_one(k, _):
        to_col(k, one_send, one_all, one_s, one_r).wait()
        return 0

    lax.fori_loop(1, COLS, wait_couple, 0)
    to_scalar = pltpu.make_async_copy(lists_all, lists_s, local)
    to_scalar.start()
    to_scalar.wait()
    lax.fori_loop(1, ROWS, wait_two, 0)

    def share(k, _):
        peer = lax.rem(c + k, COLS)
        for s in range(16):
            node = lists_s[peer, 0, s]
            at = jnp.where(lax.rem(node, COLS) == c, node // COLS, ROWS)
            v = two_all[at]
            chosen[s * 32 : s * 32 + 16] = v[:, :64]
            chosen[s * 32 + 16 : s * 32 + 32] = v[:, 64:]
        part = mm(ctwo_all[peer], chosen[...])
        part_send[k] = jnp.concatenate([part[:16], part[16:]], axis=1)
        return 0

    def part_copy(k):
        return to_col(k, part_send.at[k], part_all, part_s, part_r)

    def share_and_send(k, _):
        share(k, 0)
        part_copy(k).start()
        return 0

    lax.fori_loop(1, COLS, share_and_send, 0, unroll=True)
    share(0, 0)
    part_all[c] = part_send[0]

    lax.fori_loop(1, COLS, wait_one, 0)
    start = r * 64

    def couple(n, _):
        for s in range(12):
            node = list_one[n, s]
            p = jnp.clip(node - start, 0, 63)
            at = jnp.where(node >= 0, p // 8, COLS)
            v = one_all[at, lax.rem(p, 8) // 2]
            chosen[s * 32 : s * 32 + 32] = jnp.where(lax.rem(p, 2) == 1, v[:, 64:], v[:, :64])
        wide = jnp.concatenate([c_one[n, s] for s in range(12)], axis=1)
        field[n] = mm(wide, chosen[0:384])
        return 0

    lax.fori_loop(0, 8, couple, 0, unroll=True)

    for copy in x_halo:
        copy.wait()
    for copy in corners:
        copy.start()

    def beside_x(i, _):
        prepare(1 + i, 0)
        prepare(1 + i, 5)
        return 0

    lax.fori_loop(0, 4, beside_x, 0, unroll=True)
    lax.fori_loop(8, 12, unit_step, 0)

    def wait_part(k, _):
        part_copy(k).wait()
        return 0

    lax.fori_loop(1, COLS, wait_part, 0)
    part = part_all[0]
    for k in range(1, COLS):
        part = part + part_all[k]
    top = jnp.concatenate([part[:, :64], part[:, 64:]], axis=0)
    top_high = top.astype(BF16)
    top_low = (top - top_high.astype(F32)).astype(BF16)

    def lower(n, _):
        rows = pl.ds(pl.multiple_of(n * 32, 32), 32)
        t = t_two[rows]
        one = field[n] + mm(t, top_high) + mm(t, top_low)
        high = one.astype(BF16)
        rest = (one - high.astype(F32)).astype(BF16)
        coef[n] = (mm(t_one[n], high) + mm(t_one[n], rest)).astype(BF16)
        return 0

    lax.fori_loop(0, 8, lower, 0, unroll=True)

    def finish(i, _):
        x1, y = i // 4, lax.rem(i, 4)
        even, odd = 2 * x1 * 4 + y, (2 * x1 + 1) * 4 + y
        for h in range(2):
            at = slice(h * 128, h * 128 + 128)
            a, b = near[even, :, at], near[odd, :, at]
            for z0 in range(2):
                tile = lax.rem(y, 2) + 2 * z0 + 4 * x1 + 8 * (y // 2) + 16 * h
                rows = pl.ds(pl.multiple_of(lax.rem(tile, 4) * 64, 64), 64)
                far = mm(coef[tile // 4, rows], split_basis[tile], TN)
                lanes = pl.ds(pl.multiple_of(tile * 128, 128), 128)
                out[:, lanes] = (halves(a, b, z0) * SCALE + far).astype(BF16)
        return 0

    for copy in corners:
        copy.wait()
    for y in (0, 5):
        for x in (0, 5):
            prepare(y, x)
    lax.fori_loop(12, 16, unit_step, 0)
    lax.fori_loop(0, 8, finish, 0, unroll=True)


def shards(charges, points, leaf_basis, transfer_one, transfer_two, couple_one, couple_two, near_list, list_one, list_two):
    vmem = pl.BlockSpec(memory_space=pltpu.VMEM)
    smem = pl.BlockSpec(memory_space=pltpu.SMEM)
    dma = pltpu.SemaphoreType.DMA
    return pl.pallas_call(
        body,
        out_shape=jax.ShapeDtypeStruct(charges.shape, BF16),
        in_specs=[vmem] * 8 + [smem, vmem, vmem],
        out_specs=vmem,
        scratch_shapes=[
            pltpu.VMEM((6, 6, 64, 256), BF16),
            pltpu.VMEM((6, 6, 4, 256), F32),
            pltpu.VMEM((36, 64, 512), BF16),
            pltpu.VMEM((36, 24, 128), F32),
            pltpu.VMEM((16, 4, 320, 128), F32),
            pltpu.VMEM((9, 128, 128), F32),
            pltpu.VMEM((8, 128), F32),
            pltpu.VMEM((16, 64, 256), F32),
            pltpu.VMEM((32, 64, 128), BF16),
            pltpu.VMEM((8, 256, 64), BF16),
            pltpu.VMEM((4, 32, 128), BF16),
            pltpu.VMEM((9, 4, 32, 128), BF16),
            pltpu.VMEM((16, 128), BF16),
            pltpu.VMEM((33, 16, 128), BF16),
            pltpu.VMEM((32, 512), BF16),
            pltpu.VMEM((8, 32, 512), BF16),
            pltpu.VMEM((8, 128), jnp.int32),
            pltpu.VMEM((8, 8, 128), jnp.int32),
            pltpu.SMEM((8, 8, 128), jnp.int32),
            pltpu.VMEM((512, 64), BF16),
            pltpu.VMEM((8, 32, 64), F32),
            pltpu.VMEM((8, 16, 128), F32),
            pltpu.VMEM((8, 16, 128), F32),
            dma((16,)),
            dma((16,)),
            dma((COLS,)),
            dma((COLS,)),
            dma((ROWS,)),
            dma((ROWS,)),
            dma((COLS,)),
            dma((COLS,)),
            dma((COLS,)),
            dma((COLS,)),
            dma((COLS,)),
            dma((COLS,)),
            dma,
        ],
        compiler_params=pltpu.CompilerParams(
            collective_id=0, has_side_effects=True, vmem_limit_bytes=58 * 2**20
        ),
    )(
        charges,
        points,
        leaf_basis,
        transfer_one.reshape(8, 256, 32),
        transfer_two.reshape(256, 32),
        couple_one,
        couple_two.reshape(16, 32, 32),
        near_list.T,
        list_one,
        list_two,
        jnp.asarray(picks(), BF16),
    )


def solution(mesh):
    lead = ("row", "col")
    columns, three = P(None, lead), P(lead, None, None)
    four, two = P(lead, None, None, None), P(lead, None)
    in_specs = (columns, columns, columns, three, three, four, four, two, two, two)
    return jax.shard_map(shards, mesh=mesh, in_specs=in_specs, out_specs=columns, check_vma=False)
```

```python
import jax
import jax.numpy as jnp
import numpy as np
from jax import lax
from jax.experimental import pallas as pl
from jax.experimental.pallas import tpu as pltpu
from jax.sharding import PartitionSpec as P

F32 = jnp.float32
BF16 = jnp.bfloat16
MESH = pl.DeviceIdType.MESH
NT = (((1,), (1,)), ((), ()))
TN = (((0,), (0,)), ((), ()))
NN = (((1,), (0,)), ((), ()))

ROWS = 32
COLS = 8
SOFT = 0.0025
SCALE = (27 * 64) ** (-0.5)


def mm(a, b, dims=NN):
    return lax.dot_general(a, b, dims, preferred_element_type=F32)


def picks():
    pick = np.zeros((256, 192), np.float32)
    sides = (((0, 1, 1, 2, 3), (0, -1, 1, 0, -1)), ((0, 1, 2, 2, 3), (1, 0, -1, 1, 0)))
    for side, (places, steps) in enumerate(sides):
        for x in range(4):
            for y in range(4):
                for tile in range(5):
                    z = places[tile]
                    leaf = x % 2 + 2 * (y % 2) + 4 * (z % 2) + 8 * (x // 2) + 16 * (y // 2) + 32 * (z // 2)
                    pick[side * 128 + (x * 4 + y) * 8 + tile, (steps[tile] + 1) * 64 + leaf] = 1
    return pick


def body(
    charges,
    points,
    basis,
    t_packed,
    t_two,
    c_one,
    c_two,
    near_list,
    list_one,
    list_two,
    pick,
    out,
    ext_c,
    ext_p,
    wide_c,
    src_f,
    own_f,
    masks,
    t_flat,
    t_one,
    near,
    split_basis,
    coef,
    one_send,
    one_all,
    two_send,
    two_all,
    ctwo_send,
    ctwo_all,
    lists_send,
    lists_all,
    lists_s,
    chosen,
    field,
    part_send,
    part_all,
    halo_s,
    halo_r,
    one_s,
    one_r,
    two_s,
    two_r,
    ctwo_s,
    ctwo_r,
    lt_s,
    lt_r,
    part_s,
    part_r,
    local,
):
    r = lax.axis_index("row")
    c = lax.axis_index("col")
    barrier = pltpu.get_barrier_semaphore()

    def greet_col(k, _):
        pl.semaphore_signal(barrier, inc=1, device_id=(r, lax.rem(c + k, COLS)), device_id_type=MESH)
        return 0

    layer, spot = r // 4, lax.rem(r, 4)

    def quad_peer(k):
        return (layer * 4 + lax.rem(spot + k, 4), c)

    def ring_peer(k):
        return (lax.rem(layer + k, 8) * 4 + spot, c)

    def greet_ring(k, _):
        pl.semaphore_signal(barrier, inc=1, device_id=ring_peer(k), device_id_type=MESH)
        return 0

    lax.fori_loop(1, COLS, greet_col, 0)
    lax.fori_loop(1, 8, greet_ring, 0)
    up, down = (lax.rem(r + 1, ROWS), c), (lax.rem(r + ROWS - 1, ROWS), c)
    for peer in (quad_peer(1), quad_peer(2), quad_peer(3), up, down):
        pl.semaphore_signal(barrier, inc=1, device_id=peer, device_id_type=MESH)

    low = lax.broadcasted_iota(jnp.int32, (64, 128), 1) < 64

    def halves(a, b, upper):
        if upper:
            return jnp.concatenate([a[:, 64:], b[:, 64:]], axis=1)
        return jnp.concatenate([a[:, :64], b[:, :64]], axis=1)

    def arrange(i, _):
        x1, y = i // 4, lax.rem(i, 4)
        for h in range(2):
            tile = lax.rem(y, 2) + 4 * x1 + 8 * (y // 2) + 16 * h
            first = pl.ds(pl.multiple_of(tile * 128, 128), 128)
            second = pl.ds(pl.multiple_of(tile * 128 + 256, 128), 128)
            at = slice(h * 128, h * 128 + 128)
            a, b = charges[:, first], charges[:, second]
            pa, pb = points[:, first], points[:, second]
            for x0 in range(2):
                ext_c[1 + y, 1 + 2 * x1 + x0, :, at] = halves(a, b, x0)
                ext_p[1 + y, 1 + 2 * x1 + x0, 0:3, at] = halves(pa, pb, x0)
                ext_p[1 + y, 1 + 2 * x1 + x0, 3:4, at] = jnp.zeros((1, 128), F32)
        return 0

    lax.fori_loop(0, 8, arrange, 0, unroll=True)

    ctwo_send[...] = jnp.concatenate([c_two[s] for s in range(16)], axis=1)
    lists_send[...] = jnp.zeros_like(lists_send)
    lists_send[0:1, 0:16] = list_two[...]

    pl.semaphore_wait(barrier, COLS - 1 + 7 + 5)

    def halo(n, ref, src, dst, device):
        return pltpu.make_async_remote_copy(
            src_ref=ref.at[src],
            dst_ref=ref.at[dst],
            send_sem=halo_s.at[n],
            recv_sem=halo_r.at[n],
            device_id=device,
            device_id_type=MESH,
        )

    right, left = (r, lax.rem(c + 1, COLS)), (r, lax.rem(c + COLS - 1, COLS))
    four = pl.ds(1, 4)
    x_halo, y_halo, corners = [], [], []
    for i, ref in enumerate((ext_c, ext_p)):
        x_halo.append(halo(8 * i + 0, ref, (four, 4), (four, 0), right))
        x_halo.append(halo(8 * i + 1, ref, (four, 1), (four, 5), left))
        y_halo.append(halo(8 * i + 2, ref, (4, four), (0, four), up))
        y_halo.append(halo(8 * i + 3, ref, (1, four), (5, four), down))
        corners.append(halo(8 * i + 4, ref, (4, 0), (0, 0), up))
        corners.append(halo(8 * i + 5, ref, (4, 5), (0, 5), up))
        corners.append(halo(8 * i + 6, ref, (1, 0), (5, 0), down))
        corners.append(halo(8 * i + 7, ref, (1, 5), (5, 5), down))
    for copy in y_halo:
        copy.start()

    def to_col(k, src, ref, send, recv):
        return pltpu.make_async_remote_copy(
            src_ref=src,
            dst_ref=ref.at[c],
            send_sem=send.at[k],
            recv_sem=recv.at[k],
            device_id=(r, lax.rem(c + k, COLS)),
            device_id_type=MESH,
        )

    def to_quad(k):
        return pltpu.make_async_remote_copy(
            src_ref=two_send,
            dst_ref=two_all.at[r],
            send_sem=two_s.at[k],
            recv_sem=two_r.at[k],
            device_id=quad_peer(k),
            device_id_type=MESH,
        )

    def to_ring(k):
        quad = two_all.at[pl.ds(layer * 4, 4)]
        return pltpu.make_async_remote_copy(
            src_ref=quad,
            dst_ref=quad,
            send_sem=two_s.at[4 + k],
            recv_sem=two_r.at[4 + k],
            device_id=ring_peer(k),
            device_id_type=MESH,
        )

    def couple_copies(k):
        return to_col(k, ctwo_send, ctwo_all, ctwo_s, ctwo_r), to_col(k, lists_send, lists_all, lt_s, lt_r)

    def start_couple(k, _):
        for copy in couple_copies(k):
            copy.start()
        return 0

    lax.fori_loop(1, COLS, start_couple, 0)
    ctwo_all[c] = ctwo_send[...]
    lists_all[c] = lists_send[...]

    for a in range(0, 32, 4):
        turned = jnp.transpose(t_packed[a * 32 : a * 32 + 128].astype(F32))
        for q in range(4):
            t_flat[pl.ds(a + q, 64, stride=32)] = turned[:, q * 32 : q * 32 + 32]
    for n in range(8):
        t_one[n] = t_flat[n * 256 : n * 256 + 256].astype(BF16)

    for tile in range(32):
        b = basis[:, tile * 128 : tile * 128 + 128]
        zero = jnp.zeros((32, 64), BF16)
        split_basis[tile] = jnp.concatenate(
            [jnp.concatenate([b[:, :64], zero], axis=1), jnp.concatenate([zero, b[:, 64:]], axis=1)], axis=0
        )

    def lift(n, _):
        for i in range(4):
            lanes = pl.ds(pl.multiple_of(n * 512 + i * 128, 128), 128)
            coef[n, i * 64 : i * 64 + 64] = mm(split_basis[n * 4 + i], charges[:, lanes], NT).astype(BF16)
        field[n] = mm(t_one[n], coef[n], TN)
        return 0

    lax.fori_loop(0, 8, lift, 0, unroll=True)
    ones = [field[n].astype(BF16) for n in range(8)]
    for i in range(4):
        one_send[i] = jnp.concatenate([ones[2 * i], ones[2 * i + 1]], axis=1)
    two = mm(t_two[...], jnp.concatenate(ones, axis=0), TN).astype(BF16)
    two_send[...] = jnp.concatenate([two[:16], two[16:]], axis=1)

    def start_ring(k, _):
        to_ring(k).start()
        return 0

    def start_one(k, _):
        to_col(k, one_send, one_all, one_s, one_r).start()
        return 0

    for k in (1, 2, 3):
        to_quad(k).start()
    lax.fori_loop(1, COLS, start_one, 0)
    for copy in x_halo:
        copy.start()
    one_all[c] = one_send[...]
    one_all[COLS] = jnp.zeros((4, 32, 128), BF16)
    two_all[r] = two_send[...]
    two_all[ROWS] = jnp.zeros((16, 128), BF16)

    active = jnp.transpose(jnp.where(near_list[...] >= 0, 1.0, 0.0))
    lists = jnp.concatenate([active[:, 0:9], active[:, 9:18], active[:, 18:27]], axis=0).astype(BF16)
    blocked = jnp.where(mm(pick[...], lists) > 0.5, 0.0, jnp.inf)
    low2 = lax.broadcasted_iota(jnp.int32, (128, 128), 1) < 64
    for j in range(9):
        masks[j] = jnp.where(low2, blocked[0:128, j : j + 1], blocked[128:256, j : j + 1])

    coord = lax.broadcasted_iota(jnp.int32, (4, 256), 0)
    middle = jnp.where(coord == 0, 4 * c + 2, jnp.where(coord == 1, 4 * r + 2, jnp.where(coord == 2, 2, 0))).astype(F32)

    def prepare(y, x):
        p = ext_p[y, x] - middle
        q = p * p
        size = q[0:1] + q[1:2] + q[2:3]
        f = jnp.concatenate([-2.0 * p[0:3], size, jnp.zeros((4, 256), F32)], axis=0)
        e = y * 6 + x
        f0, f1 = f[:, :128], f[:, 128:]
        src_f[e, 0:8] = f0
        src_f[e, 8:16] = jnp.where(low[:8], f1, f0)
        src_f[e, 16:24] = f1
        ch = ext_c[y, x]
        c0, c1 = ch[:, :128], ch[:, 128:]
        zero = jnp.zeros((64, 64), BF16)
        wide_c[e, :, 0:128] = c0
        wide_c[e, :, 128:256] = jnp.concatenate([c1[:, :64], zero], axis=1)
        wide_c[e, :, 256:384] = c1
        wide_c[e, :, 384:512] = jnp.concatenate([zero, c0[:, 64:]], axis=1)
        return p, size

    def own_column(i, _):
        x, y = i // 4, lax.rem(i, 4)
        p, size = prepare(1 + y, 1 + x)
        features = (p[0:1], p[1:2], p[2:3], size + SOFT)
        for f, row in enumerate(features):
            for h in range(2):
                half = jnp.broadcast_to(row[:, h * 128 : h * 128 + 128], (128, 128))
                own_f[i, f, h * 128 : h * 128 + 128] = jnp.transpose(half)
            own_f[i, f, 256:320] = jnp.where(low, own_f[i, f, 64:128], own_f[i, f, 128:192])
        return 0

    lax.fori_loop(0, 16, own_column, 0, unroll=2)

    def unit(i):
        g, k = i // 4, lax.rem(i, 4)
        gx, gy, a, b = g // 2, lax.rem(g, 2), k // 2, lax.rem(k, 2)
        x = (1 - gx) * (1 + a) + gx * 3 * a
        y = (1 - gy) * (1 + b) + gy * 3 * b
        d = x * 4 + y
        total = [jnp.zeros((128, 64), F32), jnp.zeros((128, 64), F32)]
        zero = jnp.zeros((64, 128), BF16)
        for j in range(9):
            e = (y + j // 3) * 6 + x + j % 3
            rows = pl.ds(pl.multiple_of(d * 8, 8), 8)
            s0, sm, s1 = src_f[e, 0:8], src_f[e, 8:16], src_f[e, 16:24]
            m = masks[j, rows]

            def tile(t, first, s):
                dist = own_f[d, 3, first : first + 64] + (s[3:4] + m[t : t + 1])
                for f in range(3):
                    dist = dist + own_f[d, f, first : first + 64] * s[f : f + 1]
                return lax.rsqrt(dist.astype(BF16))

            mid = tile(2, 256, sm)
            k0 = jnp.concatenate(
                [jnp.concatenate([tile(0, 0, s0), zero], 1), jnp.concatenate([tile(1, 64, s0), mid], 1)], 0
            )
            k1 = jnp.concatenate(
                [jnp.concatenate([tile(3, 128, s1), mid], 1), jnp.concatenate([tile(4, 192, s1), zero], 1)], 0
            )
            total[0] = total[0] + mm(k0, wide_c[e, :, 0:256], NT)
            total[1] = total[1] + mm(k1, wide_c[e, :, 256:512], NT)
        near[d, :, 0:128] = jnp.transpose(total[0])
        near[d, :, 128:256] = jnp.transpose(total[1])

    def unit_step(i, _):
        unit(i)
        return 0

    for k in (1, 2, 3):
        to_quad(k).wait()
    lax.fori_loop(1, 8, start_ring, 0)
    lax.fori_loop(0, 4, unit_step, 0)

    for copy in y_halo:
        copy.wait()

    def beside_y(i, _):
        prepare(0, 1 + i)
        prepare(5, 1 + i)
        return 0

    lax.fori_loop(0, 4, beside_y, 0, unroll=True)
    lax.fori_loop(4, 8, unit_step, 0)

    def wait_couple(k, _):
        for copy in couple_copies(k):
            copy.wait()
        return 0

    def wait_ring(k, _):
        to_ring(k).wait()
        return 0

    def wait_one(k, _):
        to_col(k, one_send, one_all, one_s, one_r).wait()
        return 0

    lax.fori_loop(1, COLS, wait_couple, 0)
    to_scalar = pltpu.make_async_copy(lists_all, lists_s, local)
    to_scalar.start()
    to_scalar.wait()
    lax.fori_loop(1, 8, wait_ring, 0)

    def share(k, _):
        peer = lax.rem(c + k, COLS)
        for s in range(16):
            node = lists_s[peer, 0, s]
            at = jnp.where(lax.rem(node, COLS) == c, node // COLS, ROWS)
            v = two_all[at]
            chosen[s * 32 : s * 32 + 16] = v[:, :64]
            chosen[s * 32 + 16 : s * 32 + 32] = v[:, 64:]
        part = mm(ctwo_all[peer], chosen[...])
        part_send[k] = jnp.concatenate([part[:16], part[16:]], axis=1)
        return 0

    def part_copy(k):
        return to_col(k, part_send.at[k], part_all, part_s, part_r)

    def share_and_send(k, _):
        share(k, 0)
        part_copy(k).start()
        return 0

    lax.fori_loop(1, COLS, share_and_send, 0, unroll=True)
    share(0, 0)
    part_all[c] = part_send[0]

    lax.fori_loop(1, COLS, wait_one, 0)
    start = r * 64

    def couple(n, _):
        for s in range(12):
            node = list_one[n, s]
            p = jnp.clip(node - start, 0, 63)
            at = jnp.where(node >= 0, p // 8, COLS)
            v = one_all[at, lax.rem(p, 8) // 2]
            chosen[s * 32 : s * 32 + 32] = jnp.where(lax.rem(p, 2) == 1, v[:, 64:], v[:, :64])
        wide = jnp.concatenate([c_one[n, s] for s in range(12)], axis=1)
        field[n] = mm(wide, chosen[0:384])
        return 0

    lax.fori_loop(0, 8, couple, 0, unroll=True)

    for copy in x_halo:
        copy.wait()
    for copy in corners:
        copy.start()

    def beside_x(i, _):
        prepare(1 + i, 0)
        prepare(1 + i, 5)
        return 0

    lax.fori_loop(0, 4, beside_x, 0, unroll=True)
    lax.fori_loop(8, 12, unit_step, 0)

    def wait_part(k, _):
        part_copy(k).wait()
        return 0

    lax.fori_loop(1, COLS, wait_part, 0)
    part = part_all[0]
    for k in range(1, COLS):
        part = part + part_all[k]
    top = jnp.concatenate([part[:, :64], part[:, 64:]], axis=0)
    top_high = top.astype(BF16)
    top_low = (top - top_high.astype(F32)).astype(BF16)

    def lower(n, _):
        rows = pl.ds(pl.multiple_of(n * 32, 32), 32)
        t = t_two[rows]
        one = field[n] + mm(t, top_high) + mm(t, top_low)
        high = one.astype(BF16)
        rest = (one - high.astype(F32)).astype(BF16)
        coef[n] = (mm(t_one[n], high) + mm(t_one[n], rest)).astype(BF16)
        return 0

    lax.fori_loop(0, 8, lower, 0, unroll=True)

    def finish(i, _):
        x1, y = i // 4, lax.rem(i, 4)
        even, odd = 2 * x1 * 4 + y, (2 * x1 + 1) * 4 + y
        for h in range(2):
            at = slice(h * 128, h * 128 + 128)
            a, b = near[even, :, at], near[odd, :, at]
            for z0 in range(2):
                tile = lax.rem(y, 2) + 2 * z0 + 4 * x1 + 8 * (y // 2) + 16 * h
                rows = pl.ds(pl.multiple_of(lax.rem(tile, 4) * 64, 64), 64)
                far = mm(coef[tile // 4, rows], split_basis[tile], TN)
                lanes = pl.ds(pl.multiple_of(tile * 128, 128), 128)
                out[:, lanes] = (halves(a, b, z0) * SCALE + far).astype(BF16)
        return 0

    for copy in corners:
        copy.wait()
    for y in (0, 5):
        for x in (0, 5):
            prepare(y, x)
    lax.fori_loop(12, 16, unit_step, 0)
    lax.fori_loop(0, 8, finish, 0, unroll=True)


def shards(charges, points, leaf_basis, transfer_one, transfer_two, couple_one, couple_two, near_list, list_one, list_two):
    vmem = pl.BlockSpec(memory_space=pltpu.VMEM)
    smem = pl.BlockSpec(memory_space=pltpu.SMEM)
    dma = pltpu.SemaphoreType.DMA
    return pl.pallas_call(
        body,
        out_shape=jax.ShapeDtypeStruct(charges.shape, BF16),
        in_specs=[vmem] * 8 + [smem, vmem, vmem],
        out_specs=vmem,
        scratch_shapes=[
            pltpu.VMEM((6, 6, 64, 256), BF16),
            pltpu.VMEM((6, 6, 4, 256), F32),
            pltpu.VMEM((36, 64, 512), BF16),
            pltpu.VMEM((36, 24, 128), F32),
            pltpu.VMEM((16, 4, 320, 128), F32),
            pltpu.VMEM((9, 128, 128), F32),
            pltpu.VMEM((2048, 32), F32),
            pltpu.VMEM((8, 256, 32), BF16),
            pltpu.VMEM((16, 64, 256), F32),
            pltpu.VMEM((32, 64, 128), BF16),
            pltpu.VMEM((8, 256, 64), BF16),
            pltpu.VMEM((4, 32, 128), BF16),
            pltpu.VMEM((9, 4, 32, 128), BF16),
            pltpu.VMEM((16, 128), BF16),
            pltpu.VMEM((33, 16, 128), BF16),
            pltpu.VMEM((32, 512), BF16),
            pltpu.VMEM((8, 32, 512), BF16),
            pltpu.VMEM((8, 128), jnp.int32),
            pltpu.VMEM((8, 8, 128), jnp.int32),
            pltpu.SMEM((8, 8, 128), jnp.int32),
            pltpu.VMEM((512, 64), BF16),
            pltpu.VMEM((8, 32, 64), F32),
            pltpu.VMEM((8, 16, 128), F32),
            pltpu.VMEM((8, 16, 128), F32),
            dma((16,)),
            dma((16,)),
            dma((COLS,)),
            dma((COLS,)),
            dma((12,)),
            dma((12,)),
            dma((COLS,)),
            dma((COLS,)),
            dma((COLS,)),
            dma((COLS,)),
            dma((COLS,)),
            dma((COLS,)),
            dma,
        ],
        compiler_params=pltpu.CompilerParams(
            collective_id=0, has_side_effects=True, vmem_limit_bytes=58 * 2**20
        ),
    )(
        charges,
        points,
        leaf_basis,
        transfer_one.transpose(1, 2, 0).reshape(1024, 64),
        transfer_two.reshape(256, 32),
        couple_one,
        couple_two.reshape(16, 32, 32),
        near_list.T,
        list_one,
        list_two,
        jnp.asarray(picks(), BF16),
    )


def solution(mesh):
    lead = ("row", "col")
    columns, three = P(None, lead), P(lead, None, None)
    four, two = P(lead, None, None, None), P(lead, None)
    in_specs = (columns, columns, columns, three, three, four, four, two, two, two)
    return jax.shard_map(shards, mesh=mesh, in_specs=in_specs, out_specs=columns, check_vma=False)
```

```python
import jax
import jax.numpy as jnp
import numpy as np
from jax import lax
from jax.experimental import pallas as pl
from jax.experimental.pallas import tpu as pltpu
from jax.sharding import PartitionSpec as P

F32 = jnp.float32
BF16 = jnp.bfloat16
MESH = pl.DeviceIdType.MESH
NT = (((1,), (1,)), ((), ()))
TN = (((0,), (0,)), ((), ()))
NN = (((1,), (0,)), ((), ()))

ROWS = 32
COLS = 8
SOFT = 0.0025
SCALE = (27 * 64) ** (-0.5)


def mm(a, b, dims=NN):
    return lax.dot_general(a, b, dims, preferred_element_type=F32)


def picks():
    pick = np.zeros((256, 192), np.float32)
    sides = (((0, 1, 1, 2, 3), (0, -1, 1, 0, -1)), ((0, 1, 2, 2, 3), (1, 0, -1, 1, 0)))
    for side, (places, steps) in enumerate(sides):
        for x in range(4):
            for y in range(4):
                for tile in range(5):
                    z = places[tile]
                    leaf = x % 2 + 2 * (y % 2) + 4 * (z % 2) + 8 * (x // 2) + 16 * (y // 2) + 32 * (z // 2)
                    pick[side * 128 + (x * 4 + y) * 8 + tile, (steps[tile] + 1) * 64 + leaf] = 1
    return pick


def body(
    charges,
    points,
    basis,
    t_packed,
    t_two,
    c_one,
    c_two,
    near_list,
    list_one,
    list_two,
    pick,
    out,
    ext_c,
    ext_p,
    wide_c,
    src_f,
    own_f,
    masks,
    t_flat,
    t_one,
    near,
    split_basis,
    coef,
    one_all,
    two_send,
    two_all,
    ctwo_all,
    lists_all,
    lists_s,
    chosen,
    field,
    part_send,
    part_all,
    halo_s,
    halo_r,
    one_s,
    one_r,
    two_s,
    two_r,
    ctwo_s,
    ctwo_r,
    lt_s,
    lt_r,
    part_s,
    part_r,
    local,
):
    r = lax.axis_index("row")
    c = lax.axis_index("col")
    barrier = pltpu.get_barrier_semaphore()

    def greet_col(k, _):
        pl.semaphore_signal(barrier, inc=1, device_id=(r, lax.rem(c + k, COLS)), device_id_type=MESH)
        return 0

    layer, spot = r // 4, lax.rem(r, 4)

    def quad_peer(k):
        return (layer * 4 + lax.rem(spot + k, 4), c)

    def ring_peer(k):
        return (lax.rem(layer + k, 8) * 4 + spot, c)

    def greet_ring(k, _):
        pl.semaphore_signal(barrier, inc=1, device_id=ring_peer(k), device_id_type=MESH)
        return 0

    lax.fori_loop(1, COLS, greet_col, 0)
    lax.fori_loop(1, 8, greet_ring, 0)
    up, down = (lax.rem(r + 1, ROWS), c), (lax.rem(r + ROWS - 1, ROWS), c)
    for peer in (quad_peer(1), quad_peer(2), quad_peer(3), up, down):
        pl.semaphore_signal(barrier, inc=1, device_id=peer, device_id_type=MESH)

    low = lax.broadcasted_iota(jnp.int32, (64, 128), 1) < 64

    def halves(a, b, upper):
        if upper:
            return jnp.concatenate([a[:, 64:], b[:, 64:]], axis=1)
        return jnp.concatenate([a[:, :64], b[:, :64]], axis=1)

    def arrange(i, _):
        x1, y = i // 4, lax.rem(i, 4)
        for h in range(2):
            tile = lax.rem(y, 2) + 4 * x1 + 8 * (y // 2) + 16 * h
            first = pl.ds(pl.multiple_of(tile * 128, 128), 128)
            second = pl.ds(pl.multiple_of(tile * 128 + 256, 128), 128)
            at = slice(h * 128, h * 128 + 128)
            a, b = charges[:, first], charges[:, second]
            pa, pb = points[:, first], points[:, second]
            for x0 in range(2):
                ext_c[1 + y, 1 + 2 * x1 + x0, :, at] = halves(a, b, x0)
                ext_p[1 + y, 1 + 2 * x1 + x0, 0:3, at] = halves(pa, pb, x0)
                ext_p[1 + y, 1 + 2 * x1 + x0, 3:4, at] = jnp.zeros((1, 128), F32)
        return 0

    lax.fori_loop(0, 8, arrange, 0, unroll=True)

    ctwo_all[c] = jnp.concatenate([c_two[s] for s in range(16)], axis=1)
    lists_all[c] = jnp.zeros((8, 128), jnp.int32)
    lists_all[c, 0:1, 0:16] = list_two[...]

    pl.semaphore_wait(barrier, COLS - 1 + 7 + 5)

    def halo(n, ref, src, dst, device):
        return pltpu.make_async_remote_copy(
            src_ref=ref.at[src],
            dst_ref=ref.at[dst],
            send_sem=halo_s.at[n],
            recv_sem=halo_r.at[n],
            device_id=device,
            device_id_type=MESH,
        )

    right, left = (r, lax.rem(c + 1, COLS)), (r, lax.rem(c + COLS - 1, COLS))
    four = pl.ds(1, 4)
    x_halo, y_halo, corners = [], [], []
    for i, ref in enumerate((ext_c, ext_p)):
        x_halo.append(halo(8 * i + 0, ref, (four, 4), (four, 0), right))
        x_halo.append(halo(8 * i + 1, ref, (four, 1), (four, 5), left))
        y_halo.append(halo(8 * i + 2, ref, (4, four), (0, four), up))
        y_halo.append(halo(8 * i + 3, ref, (1, four), (5, four), down))
        corners.append(halo(8 * i + 4, ref, (4, 0), (0, 0), up))
        corners.append(halo(8 * i + 5, ref, (4, 5), (0, 5), up))
        corners.append(halo(8 * i + 6, ref, (1, 0), (5, 0), down))
        corners.append(halo(8 * i + 7, ref, (1, 5), (5, 5), down))

    def to_col(k, src, ref, send, recv):
        return pltpu.make_async_remote_copy(
            src_ref=src,
            dst_ref=ref.at[c],
            send_sem=send.at[k],
            recv_sem=recv.at[k],
            device_id=(r, lax.rem(c + k, COLS)),
            device_id_type=MESH,
        )

    def to_quad(k):
        return pltpu.make_async_remote_copy(
            src_ref=two_send,
            dst_ref=two_all.at[r],
            send_sem=two_s.at[k],
            recv_sem=two_r.at[k],
            device_id=quad_peer(k),
            device_id_type=MESH,
        )

    def to_ring(k):
        quad = two_all.at[pl.ds(layer * 4, 4)]
        return pltpu.make_async_remote_copy(
            src_ref=quad,
            dst_ref=quad,
            send_sem=two_s.at[4 + k],
            recv_sem=two_r.at[4 + k],
            device_id=ring_peer(k),
            device_id_type=MESH,
        )

    far_y = c + 1 - 2 * lax.rem(c, 2)
    place = c // 2

    def across(ref, send, recv):
        return pltpu.make_async_remote_copy(
            src_ref=ref.at[c],
            dst_ref=ref.at[c],
            send_sem=send.at[0],
            recv_sem=recv.at[0],
            device_id=(r, far_y),
            device_id_type=MESH,
        )

    def along(k, ref, send, recv):
        both = ref.at[pl.ds(place * 2, 2)]
        return pltpu.make_async_remote_copy(
            src_ref=both,
            dst_ref=both,
            send_sem=send.at[k],
            recv_sem=recv.at[k],
            device_id=(r, lax.rem(place + k, 4) * 2 + lax.rem(c, 2)),
            device_id_type=MESH,
        )

    gathers = ((ctwo_all, ctwo_s, ctwo_r), (lists_all, lt_s, lt_r), (one_all, one_s, one_r))

    for gather in gathers[:2]:
        across(*gather).start()
    for copy in y_halo + x_halo:
        copy.start()

    for a in range(0, 32, 4):
        turned = jnp.transpose(t_packed[a * 32 : a * 32 + 128].astype(F32))
        for q in range(4):
            t_flat[pl.ds(a + q, 64, stride=32)] = turned[:, q * 32 : q * 32 + 32]
    for n in range(8):
        t_one[n] = t_flat[n * 256 : n * 256 + 256].astype(BF16)

    for tile in range(32):
        b = basis[:, tile * 128 : tile * 128 + 128]
        zero = jnp.zeros((32, 64), BF16)
        split_basis[tile] = jnp.concatenate(
            [jnp.concatenate([b[:, :64], zero], axis=1), jnp.concatenate([zero, b[:, 64:]], axis=1)], axis=0
        )

    def lift(n, _):
        for i in range(4):
            lanes = pl.ds(pl.multiple_of(n * 512 + i * 128, 128), 128)
            coef[n, i * 64 : i * 64 + 64] = mm(split_basis[n * 4 + i], charges[:, lanes], NT).astype(BF16)
        field[n] = mm(t_one[n], coef[n], TN)
        return 0

    lax.fori_loop(0, 8, lift, 0, unroll=True)
    ones = [field[n].astype(BF16) for n in range(8)]
    for i in range(4):
        one_all[c, i] = jnp.concatenate([ones[2 * i], ones[2 * i + 1]], axis=1)
    two = mm(t_two[...], jnp.concatenate(ones, axis=0), TN).astype(BF16)
    two_send[...] = jnp.concatenate([two[:16], two[16:]], axis=1)

    def start_ring(k, _):
        to_ring(k).start()
        return 0

    for k in (1, 2, 3):
        to_quad(k).start()
    across(*gathers[2]).start()
    for gather in gathers[:2]:
        across(*gather).wait()
        for k in (1, 2, 3):
            along(k, *gather).start()
    one_all[COLS] = jnp.zeros((4, 32, 128), BF16)
    two_all[r] = two_send[...]
    two_all[ROWS] = jnp.zeros((16, 128), BF16)

    active = jnp.transpose(jnp.where(near_list[...] >= 0, 1.0, 0.0))
    lists = jnp.concatenate([active[:, 0:9], active[:, 9:18], active[:, 18:27]], axis=0).astype(BF16)
    blocked = jnp.where(mm(pick[...], lists) > 0.5, 0.0, jnp.inf)
    low2 = lax.broadcasted_iota(jnp.int32, (128, 128), 1) < 64
    for j in range(9):
        masks[j] = jnp.where(low2, blocked[0:128, j : j + 1], blocked[128:256, j : j + 1])

    coord = lax.broadcasted_iota(jnp.int32, (4, 256), 0)
    middle = jnp.where(coord == 0, 4 * c + 2, jnp.where(coord == 1, 4 * r + 2, jnp.where(coord == 2, 2, 0))).astype(F32)

    def prepare(y, x):
        p = ext_p[y, x] - middle
        q = p * p
        size = q[0:1] + q[1:2] + q[2:3]
        f = jnp.concatenate([-2.0 * p[0:3], size, jnp.zeros((4, 256), F32)], axis=0)
        e = y * 6 + x
        f0, f1 = f[:, :128], f[:, 128:]
        src_f[e, 0:8] = f0
        src_f[e, 8:16] = jnp.where(low[:8], f1, f0)
        src_f[e, 16:24] = f1
        ch = ext_c[y, x]
        c0, c1 = ch[:, :128], ch[:, 128:]
        zero = jnp.zeros((64, 64), BF16)
        wide_c[e, :, 0:128] = c0
        wide_c[e, :, 128:256] = jnp.concatenate([c1[:, :64], zero], axis=1)
        wide_c[e, :, 256:384] = c1
        wide_c[e, :, 384:512] = jnp.concatenate([zero, c0[:, 64:]], axis=1)
        return p, size

    def own_column(i, _):
        x, y = i // 4, lax.rem(i, 4)
        p, size = prepare(1 + y, 1 + x)
        features = (p[0:1], p[1:2], p[2:3], size + SOFT)
        for f, row in enumerate(features):
            for h in range(2):
                half = jnp.broadcast_to(row[:, h * 128 : h * 128 + 128], (128, 128))
                own_f[i, f, h * 128 : h * 128 + 128] = jnp.transpose(half)
            own_f[i, f, 256:320] = jnp.where(low, own_f[i, f, 64:128], own_f[i, f, 128:192])
        return 0

    lax.fori_loop(0, 16, own_column, 0, unroll=2)

    def unit(i):
        g, k = i // 4, lax.rem(i, 4)
        gx, gy, a, b = g // 2, lax.rem(g, 2), k // 2, lax.rem(k, 2)
        x = (1 - gx) * (1 + a) + gx * 3 * a
        y = (1 - gy) * (1 + b) + gy * 3 * b
        d = x * 4 + y
        total = [jnp.zeros((128, 64), F32), jnp.zeros((128, 64), F32)]
        zero = jnp.zeros((64, 128), BF16)
        for j in range(9):
            e = (y + j // 3) * 6 + x + j % 3
            rows = pl.ds(pl.multiple_of(d * 8, 8), 8)
            s0, sm, s1 = src_f[e, 0:8], src_f[e, 8:16], src_f[e, 16:24]
            m = masks[j, rows]

            def tile(t, first, s):
                dist = own_f[d, 3, first : first + 64] + (s[3:4] + m[t : t + 1])
                for f in range(3):
                    dist = dist + own_f[d, f, first : first + 64] * s[f : f + 1]
                return lax.rsqrt(dist.astype(BF16))

            mid = tile(2, 256, sm)
            k0 = jnp.concatenate(
                [jnp.concatenate([tile(0, 0, s0), zero], 1), jnp.concatenate([tile(1, 64, s0), mid], 1)], 0
            )
            k1 = jnp.concatenate(
                [jnp.concatenate([tile(3, 128, s1), mid], 1), jnp.concatenate([tile(4, 192, s1), zero], 1)], 0
            )
            total[0] = total[0] + mm(k0, wide_c[e, :, 0:256], NT)
            total[1] = total[1] + mm(k1, wide_c[e, :, 256:512], NT)
        near[d, :, 0:128] = jnp.transpose(total[0])
        near[d, :, 128:256] = jnp.transpose(total[1])

    def unit_step(i, _):
        unit(i)
        return 0

    for k in (1, 2, 3):
        to_quad(k).wait()
    lax.fori_loop(1, 8, start_ring, 0)
    across(*gathers[2]).wait()
    for k in (1, 2, 3):
        along(k, *gathers[2]).start()
    lax.fori_loop(0, 4, unit_step, 0)

    for copy in y_halo:
        copy.wait()

    def beside_y(i, _):
        prepare(0, 1 + i)
        prepare(5, 1 + i)
        return 0

    lax.fori_loop(0, 4, beside_y, 0, unroll=True)
    lax.fori_loop(4, 8, unit_step, 0)

    def wait_ring(k, _):
        to_ring(k).wait()
        return 0

    for gather in gathers[:2]:
        for k in (1, 2, 3):
            along(k, *gather).wait()
    to_scalar = pltpu.make_async_copy(lists_all, lists_s, local)
    to_scalar.start()
    to_scalar.wait()
    lax.fori_loop(1, 8, wait_ring, 0)

    def share(k, _):
        peer = lax.rem(c + k, COLS)
        for s in range(16):
            node = lists_s[peer, 0, s]
            at = jnp.where(lax.rem(node, COLS) == c, node // COLS, ROWS)
            v = two_all[at]
            chosen[s * 32 : s * 32 + 16] = v[:, :64]
            chosen[s * 32 + 16 : s * 32 + 32] = v[:, 64:]
        part = mm(ctwo_all[peer], chosen[...])
        part_send[k] = jnp.concatenate([part[:16], part[16:]], axis=1)
        return 0

    def part_copy(k):
        return to_col(k, part_send.at[k], part_all, part_s, part_r)

    def share_and_send(k, _):
        share(k, 0)
        part_copy(k).start()
        return 0

    lax.fori_loop(1, COLS, share_and_send, 0, unroll=True)
    share(0, 0)
    part_all[c] = part_send[0]

    for k in (1, 2, 3):
        along(k, *gathers[2]).wait()
    start = r * 64

    def couple(n, _):
        for s in range(12):
            node = list_one[n, s]
            p = jnp.clip(node - start, 0, 63)
            at = jnp.where(node >= 0, p // 8, COLS)
            v = one_all[at, lax.rem(p, 8) // 2]
            chosen[s * 32 : s * 32 + 32] = jnp.where(lax.rem(p, 2) == 1, v[:, 64:], v[:, :64])
        wide = jnp.concatenate([c_one[n, s] for s in range(12)], axis=1)
        field[n] = mm(wide, chosen[0:384])
        return 0

    lax.fori_loop(0, 8, couple, 0, unroll=True)

    for copy in x_halo:
        copy.wait()
    for copy in corners:
        copy.start()

    def beside_x(i, _):
        prepare(1 + i, 0)
        prepare(1 + i, 5)
        return 0

    lax.fori_loop(0, 4, beside_x, 0, unroll=True)
    lax.fori_loop(8, 12, unit_step, 0)

    def wait_part(k, _):
        part_copy(k).wait()
        return 0

    lax.fori_loop(1, COLS, wait_part, 0)
    part = part_all[0]
    for k in range(1, COLS):
        part = part + part_all[k]
    top = jnp.concatenate([part[:, :64], part[:, 64:]], axis=0)
    top_high = top.astype(BF16)
    top_low = (top - top_high.astype(F32)).astype(BF16)

    def lower(n, _):
        rows = pl.ds(pl.multiple_of(n * 32, 32), 32)
        t = t_two[rows]
        one = field[n] + mm(t, top_high) + mm(t, top_low)
        high = one.astype(BF16)
        rest = (one - high.astype(F32)).astype(BF16)
        coef[n] = (mm(t_one[n], high) + mm(t_one[n], rest)).astype(BF16)
        return 0

    lax.fori_loop(0, 8, lower, 0, unroll=True)

    def finish(i, _):
        x1, y = i // 4, lax.rem(i, 4)
        even, odd = 2 * x1 * 4 + y, (2 * x1 + 1) * 4 + y
        for h in range(2):
            at = slice(h * 128, h * 128 + 128)
            a, b = near[even, :, at], near[odd, :, at]
            for z0 in range(2):
                tile = lax.rem(y, 2) + 2 * z0 + 4 * x1 + 8 * (y // 2) + 16 * h
                rows = pl.ds(pl.multiple_of(lax.rem(tile, 4) * 64, 64), 64)
                far = mm(coef[tile // 4, rows], split_basis[tile], TN)
                lanes = pl.ds(pl.multiple_of(tile * 128, 128), 128)
                out[:, lanes] = (halves(a, b, z0) * SCALE + far).astype(BF16)
        return 0

    for copy in corners:
        copy.wait()
    for y in (0, 5):
        for x in (0, 5):
            prepare(y, x)
    lax.fori_loop(12, 16, unit_step, 0)
    lax.fori_loop(0, 8, finish, 0, unroll=True)


def shards(charges, points, leaf_basis, transfer_one, transfer_two, couple_one, couple_two, near_list, list_one, list_two):
    vmem = pl.BlockSpec(memory_space=pltpu.VMEM)
    smem = pl.BlockSpec(memory_space=pltpu.SMEM)
    dma = pltpu.SemaphoreType.DMA
    return pl.pallas_call(
        body,
        out_shape=jax.ShapeDtypeStruct(charges.shape, BF16),
        in_specs=[vmem] * 8 + [smem, vmem, vmem],
        out_specs=vmem,
        scratch_shapes=[
            pltpu.VMEM((6, 6, 64, 256), BF16),
            pltpu.VMEM((6, 6, 4, 256), F32),
            pltpu.VMEM((36, 64, 512), BF16),
            pltpu.VMEM((36, 24, 128), F32),
            pltpu.VMEM((16, 4, 320, 128), F32),
            pltpu.VMEM((9, 128, 128), F32),
            pltpu.VMEM((2048, 32), F32),
            pltpu.VMEM((8, 256, 32), BF16),
            pltpu.VMEM((16, 64, 256), F32),
            pltpu.VMEM((32, 64, 128), BF16),
            pltpu.VMEM((8, 256, 64), BF16),
            pltpu.VMEM((9, 4, 32, 128), BF16),
            pltpu.VMEM((16, 128), BF16),
            pltpu.VMEM((33, 16, 128), BF16),
            pltpu.VMEM((8, 32, 512), BF16),
            pltpu.VMEM((8, 8, 128), jnp.int32),
            pltpu.SMEM((8, 8, 128), jnp.int32),
            pltpu.VMEM((512, 64), BF16),
            pltpu.VMEM((8, 32, 64), F32),
            pltpu.VMEM((8, 16, 128), F32),
            pltpu.VMEM((8, 16, 128), F32),
            dma((16,)),
            dma((16,)),
            dma((COLS,)),
            dma((COLS,)),
            dma((12,)),
            dma((12,)),
            dma((COLS,)),
            dma((COLS,)),
            dma((COLS,)),
            dma((COLS,)),
            dma((COLS,)),
            dma((COLS,)),
            dma,
        ],
        compiler_params=pltpu.CompilerParams(
            collective_id=0, has_side_effects=True, vmem_limit_bytes=58 * 2**20
        ),
    )(
        charges,
        points,
        leaf_basis,
        transfer_one.transpose(1, 2, 0).reshape(1024, 64),
        transfer_two.reshape(256, 32),
        couple_one,
        couple_two.reshape(16, 32, 32),
        near_list.T,
        list_one,
        list_two,
        jnp.asarray(picks(), BF16),
    )


def solution(mesh):
    lead = ("row", "col")
    columns, three = P(None, lead), P(lead, None, None)
    four, two = P(lead, None, None, None), P(lead, None)
    in_specs = (columns, columns, columns, three, three, four, four, two, two, two)
    return jax.shard_map(shards, mesh=mesh, in_specs=in_specs, out_specs=columns, check_vma=False)
```

```python
import jax
import jax.numpy as jnp
import numpy as np
from jax import lax
from jax.experimental import pallas as pl
from jax.experimental.pallas import tpu as pltpu
from jax.sharding import PartitionSpec as P

F32 = jnp.float32
BF16 = jnp.bfloat16
MESH = pl.DeviceIdType.MESH
NT = (((1,), (1,)), ((), ()))
TN = (((0,), (0,)), ((), ()))
NN = (((1,), (0,)), ((), ()))

ROWS = 32
COLS = 8
SOFT = 0.0025
SCALE = (27 * 64) ** (-0.5)


def mm(a, b, dims=NN):
    return lax.dot_general(a, b, dims, preferred_element_type=F32)


def picks():
    pick = np.zeros((256, 192), np.float32)
    sides = (((0, 1, 1, 2, 3), (0, -1, 1, 0, -1)), ((0, 1, 2, 2, 3), (1, 0, -1, 1, 0)))
    for side, (places, steps) in enumerate(sides):
        for x in range(4):
            for y in range(4):
                for tile in range(5):
                    z = places[tile]
                    leaf = x % 2 + 2 * (y % 2) + 4 * (z % 2) + 8 * (x // 2) + 16 * (y // 2) + 32 * (z // 2)
                    pick[side * 128 + (x * 4 + y) * 8 + tile, (steps[tile] + 1) * 64 + leaf] = 1
    return pick


def body(
    charges,
    points,
    basis,
    t_packed,
    t_two,
    c_one,
    c_two,
    near_list,
    list_one,
    list_two,
    pick,
    out,
    ext_c,
    ext_p,
    wide_c,
    src_f,
    own_f,
    masks,
    t_flat,
    t_one,
    near,
    split_basis,
    coef,
    one_all,
    two_send,
    two_all,
    ctwo_all,
    lists_all,
    lists_s,
    chosen,
    field,
    part_send,
    part_all,
    halo_s,
    halo_r,
    one_s,
    one_r,
    two_s,
    two_r,
    ctwo_s,
    ctwo_r,
    lt_s,
    lt_r,
    part_s,
    part_r,
    local,
):
    r = lax.axis_index("row")
    c = lax.axis_index("col")
    barrier = pltpu.get_barrier_semaphore()

    def greet_col(k, _):
        pl.semaphore_signal(barrier, inc=1, device_id=(r, lax.rem(c + k, COLS)), device_id_type=MESH)
        return 0

    layer, spot = r // 4, lax.rem(r, 4)

    def quad_peer(k):
        return (layer * 4 + lax.rem(spot + k, 4), c)

    def ring_peer(k):
        return (lax.rem(layer + k, 8) * 4 + spot, c)

    def greet_ring(k, _):
        pl.semaphore_signal(barrier, inc=1, device_id=ring_peer(k), device_id_type=MESH)
        return 0

    lax.fori_loop(1, COLS, greet_col, 0)
    lax.fori_loop(1, 8, greet_ring, 0)
    up, down = (lax.rem(r + 1, ROWS), c), (lax.rem(r + ROWS - 1, ROWS), c)
    for peer in (quad_peer(1), quad_peer(2), quad_peer(3), up, down):
        pl.semaphore_signal(barrier, inc=1, device_id=peer, device_id_type=MESH)

    low = lax.broadcasted_iota(jnp.int32, (64, 128), 1) < 64

    def halves(a, b, upper):
        if upper:
            return jnp.concatenate([a[:, 64:], b[:, 64:]], axis=1)
        return jnp.concatenate([a[:, :64], b[:, :64]], axis=1)

    def arrange(i, _):
        x1, y = i // 4, lax.rem(i, 4)
        for h in range(2):
            tile = lax.rem(y, 2) + 4 * x1 + 8 * (y // 2) + 16 * h
            first = pl.ds(pl.multiple_of(tile * 128, 128), 128)
            second = pl.ds(pl.multiple_of(tile * 128 + 256, 128), 128)
            at = slice(h * 128, h * 128 + 128)
            a, b = charges[:, first], charges[:, second]
            pa, pb = points[:, first], points[:, second]
            for x0 in range(2):
                ext_c[1 + y, 1 + 2 * x1 + x0, :, at] = halves(a, b, x0)
                ext_p[1 + y, 1 + 2 * x1 + x0, 0:3, at] = halves(pa, pb, x0)
                ext_p[1 + y, 1 + 2 * x1 + x0, 3:4, at] = jnp.zeros((1, 128), F32)
        return 0

    lax.fori_loop(0, 8, arrange, 0, unroll=True)

    ctwo_all[c] = jnp.concatenate([c_two[s] for s in range(16)], axis=1)
    lists_all[c] = jnp.zeros((8, 128), jnp.int32)
    lists_all[c, 0:1, 0:16] = list_two[...]

    def halo(n, ref, src, dst, device):
        return pltpu.make_async_remote_copy(
            src_ref=ref.at[src],
            dst_ref=ref.at[dst],
            send_sem=halo_s.at[n],
            recv_sem=halo_r.at[n],
            device_id=device,
            device_id_type=MESH,
        )

    right, left = (r, lax.rem(c + 1, COLS)), (r, lax.rem(c + COLS - 1, COLS))
    four = pl.ds(1, 4)
    x_halo, y_halo, corners = [], [], []
    for i, ref in enumerate((ext_c, ext_p)):
        x_halo.append(halo(8 * i + 0, ref, (four, 4), (four, 0), right))
        x_halo.append(halo(8 * i + 1, ref, (four, 1), (four, 5), left))
        y_halo.append(halo(8 * i + 2, ref, (4, four), (0, four), up))
        y_halo.append(halo(8 * i + 3, ref, (1, four), (5, four), down))
        corners.append(halo(8 * i + 4, ref, (4, 0), (0, 0), up))
        corners.append(halo(8 * i + 5, ref, (4, 5), (0, 5), up))
        corners.append(halo(8 * i + 6, ref, (1, 0), (5, 0), down))
        corners.append(halo(8 * i + 7, ref, (1, 5), (5, 5), down))

    def to_col(k, src, ref, send, recv):
        return pltpu.make_async_remote_copy(
            src_ref=src,
            dst_ref=ref.at[c],
            send_sem=send.at[k],
            recv_sem=recv.at[k],
            device_id=(r, lax.rem(c + k, COLS)),
            device_id_type=MESH,
        )

    def to_quad(k):
        return pltpu.make_async_remote_copy(
            src_ref=two_send,
            dst_ref=two_all.at[r],
            send_sem=two_s.at[k],
            recv_sem=two_r.at[k],
            device_id=quad_peer(k),
            device_id_type=MESH,
        )

    def to_ring(k):
        quad = two_all.at[pl.ds(layer * 4, 4)]
        return pltpu.make_async_remote_copy(
            src_ref=quad,
            dst_ref=quad,
            send_sem=two_s.at[4 + k],
            recv_sem=two_r.at[4 + k],
            device_id=ring_peer(k),
            device_id_type=MESH,
        )

    far_y = c + 1 - 2 * lax.rem(c, 2)
    place = c // 2

    def across(ref, send, recv):
        return pltpu.make_async_remote_copy(
            src_ref=ref.at[c],
            dst_ref=ref.at[c],
            send_sem=send.at[0],
            recv_sem=recv.at[0],
            device_id=(r, far_y),
            device_id_type=MESH,
        )

    def along(k, ref, send, recv):
        both = ref.at[pl.ds(place * 2, 2)]
        return pltpu.make_async_remote_copy(
            src_ref=both,
            dst_ref=both,
            send_sem=send.at[k],
            recv_sem=recv.at[k],
            device_id=(r, lax.rem(place + k, 4) * 2 + lax.rem(c, 2)),
            device_id_type=MESH,
        )

    gathers = ((ctwo_all, ctwo_s, ctwo_r), (lists_all, lt_s, lt_r), (one_all, one_s, one_r))

    for a in range(0, 32, 4):
        turned = jnp.transpose(t_packed[a * 32 : a * 32 + 128].astype(F32))
        for q in range(4):
            t_flat[pl.ds(a + q, 64, stride=32)] = turned[:, q * 32 : q * 32 + 32]
    for n in range(8):
        t_one[n] = t_flat[n * 256 : n * 256 + 256].astype(BF16)

    for tile in range(32):
        b = basis[:, tile * 128 : tile * 128 + 128]
        zero = jnp.zeros((32, 64), BF16)
        split_basis[tile] = jnp.concatenate(
            [jnp.concatenate([b[:, :64], zero], axis=1), jnp.concatenate([zero, b[:, 64:]], axis=1)], axis=0
        )

    def lift(n, _):
        for i in range(4):
            lanes = pl.ds(pl.multiple_of(n * 512 + i * 128, 128), 128)
            coef[n, i * 64 : i * 64 + 64] = mm(split_basis[n * 4 + i], charges[:, lanes], NT).astype(BF16)
        field[n] = mm(t_one[n], coef[n], TN)
        return 0

    lax.fori_loop(0, 8, lift, 0, unroll=True)
    ones = [field[n].astype(BF16) for n in range(8)]
    for i in range(4):
        one_all[c, i] = jnp.concatenate([ones[2 * i], ones[2 * i + 1]], axis=1)
    two = mm(t_two[...], jnp.concatenate(ones, axis=0), TN).astype(BF16)
    two_send[...] = jnp.concatenate([two[:16], two[16:]], axis=1)

    def start_ring(k, _):
        to_ring(k).start()
        return 0

    pl.semaphore_wait(barrier, COLS - 1 + 7 + 5)
    for k in (1, 2, 3):
        to_quad(k).start()
    for gather in gathers:
        across(*gather).start()
    for copy in y_halo:
        copy.start()
    one_all[COLS] = jnp.zeros((4, 32, 128), BF16)
    two_all[r] = two_send[...]
    two_all[ROWS] = jnp.zeros((16, 128), BF16)

    active = jnp.transpose(jnp.where(near_list[...] >= 0, 1.0, 0.0))
    lists = jnp.concatenate([active[:, 0:9], active[:, 9:18], active[:, 18:27]], axis=0).astype(BF16)
    blocked = jnp.where(mm(pick[...], lists) > 0.5, 0.0, jnp.inf)
    low2 = lax.broadcasted_iota(jnp.int32, (128, 128), 1) < 64
    for j in range(9):
        masks[j] = jnp.where(low2, blocked[0:128, j : j + 1], blocked[128:256, j : j + 1])

    coord = lax.broadcasted_iota(jnp.int32, (4, 256), 0)
    middle = jnp.where(coord == 0, 4 * c + 2, jnp.where(coord == 1, 4 * r + 2, jnp.where(coord == 2, 2, 0))).astype(F32)

    def prepare(y, x):
        p = ext_p[y, x] - middle
        q = p * p
        size = q[0:1] + q[1:2] + q[2:3]
        f = jnp.concatenate([-2.0 * p[0:3], size, jnp.zeros((4, 256), F32)], axis=0)
        e = y * 6 + x
        f0, f1 = f[:, :128], f[:, 128:]
        src_f[e, 0:8] = f0
        src_f[e, 8:16] = jnp.where(low[:8], f1, f0)
        src_f[e, 16:24] = f1
        ch = ext_c[y, x]
        c0, c1 = ch[:, :128], ch[:, 128:]
        zero = jnp.zeros((64, 64), BF16)
        wide_c[e, :, 0:128] = c0
        wide_c[e, :, 128:256] = jnp.concatenate([c1[:, :64], zero], axis=1)
        wide_c[e, :, 256:384] = c1
        wide_c[e, :, 384:512] = jnp.concatenate([zero, c0[:, 64:]], axis=1)
        return p, size

    def own_column(i, _):
        x, y = i // 4, lax.rem(i, 4)
        p, size = prepare(1 + y, 1 + x)
        features = (p[0:1], p[1:2], p[2:3], size + SOFT)
        for f, row in enumerate(features):
            for h in range(2):
                half = jnp.broadcast_to(row[:, h * 128 : h * 128 + 128], (128, 128))
                own_f[i, f, h * 128 : h * 128 + 128] = jnp.transpose(half)
            own_f[i, f, 256:320] = jnp.where(low, own_f[i, f, 64:128], own_f[i, f, 128:192])
        return 0

    lax.fori_loop(0, 16, own_column, 0, unroll=2)

    def unit(i):
        g, k = i // 4, lax.rem(i, 4)
        gx, gy, a, b = g // 2, lax.rem(g, 2), k // 2, lax.rem(k, 2)
        x = (1 - gx) * (1 + a) + gx * 3 * a
        y = (1 - gy) * (1 + b) + gy * 3 * b
        d = x * 4 + y
        total = [jnp.zeros((128, 64), F32), jnp.zeros((128, 64), F32)]
        zero = jnp.zeros((64, 128), BF16)
        for j in range(9):
            e = (y + j // 3) * 6 + x + j % 3
            rows = pl.ds(pl.multiple_of(d * 8, 8), 8)
            s0, sm, s1 = src_f[e, 0:8], src_f[e, 8:16], src_f[e, 16:24]
            m = masks[j, rows]

            def tile(t, first, s):
                dist = own_f[d, 3, first : first + 64] + (s[3:4] + m[t : t + 1])
                for f in range(3):
                    dist = dist + own_f[d, f, first : first + 64] * s[f : f + 1]
                return lax.rsqrt(dist.astype(BF16))

            mid = tile(2, 256, sm)
            k0 = jnp.concatenate(
                [jnp.concatenate([tile(0, 0, s0), zero], 1), jnp.concatenate([tile(1, 64, s0), mid], 1)], 0
            )
            k1 = jnp.concatenate(
                [jnp.concatenate([tile(3, 128, s1), mid], 1), jnp.concatenate([tile(4, 192, s1), zero], 1)], 0
            )
            total[0] = total[0] + mm(k0, wide_c[e, :, 0:256], NT)
            total[1] = total[1] + mm(k1, wide_c[e, :, 256:512], NT)
        near[d, :, 0:128] = jnp.transpose(total[0])
        near[d, :, 128:256] = jnp.transpose(total[1])

    def unit_step(i, _):
        unit(i)
        return 0

    for k in (1, 2, 3):
        to_quad(k).wait()
    lax.fori_loop(1, 8, start_ring, 0)
    for gather in gathers:
        across(*gather).wait()
        for k in (1, 2, 3):
            along(k, *gather).start()
    for copy in x_halo:
        copy.start()
    lax.fori_loop(0, 4, unit_step, 0)

    for copy in y_halo:
        copy.wait()

    def beside_y(i, _):
        prepare(0, 1 + i)
        prepare(5, 1 + i)
        return 0

    lax.fori_loop(0, 4, beside_y, 0, unroll=True)
    lax.fori_loop(4, 8, unit_step, 0)

    def wait_ring(k, _):
        to_ring(k).wait()
        return 0

    for gather in gathers[:2]:
        for k in (1, 2, 3):
            along(k, *gather).wait()
    to_scalar = pltpu.make_async_copy(lists_all, lists_s, local)
    to_scalar.start()
    to_scalar.wait()
    lax.fori_loop(1, 8, wait_ring, 0)

    def share(k, _):
        peer = lax.rem(c + k, COLS)
        for s in range(16):
            node = lists_s[peer, 0, s]
            at = jnp.where(lax.rem(node, COLS) == c, node // COLS, ROWS)
            v = two_all[at]
            chosen[s * 32 : s * 32 + 16] = v[:, :64]
            chosen[s * 32 + 16 : s * 32 + 32] = v[:, 64:]
        part = mm(ctwo_all[peer], chosen[...])
        part_send[k] = jnp.concatenate([part[:16], part[16:]], axis=1)
        return 0

    def part_copy(k):
        return to_col(k, part_send.at[k], part_all, part_s, part_r)

    def share_and_send(k, _):
        share(k, 0)
        part_copy(k).start()
        return 0

    lax.fori_loop(1, COLS, share_and_send, 0, unroll=True)
    share(0, 0)
    part_all[c] = part_send[0]

    for k in (1, 2, 3):
        along(k, *gathers[2]).wait()
    start = r * 64

    def couple(n, _):
        for s in range(12):
            node = list_one[n, s]
            p = jnp.clip(node - start, 0, 63)
            at = jnp.where(node >= 0, p // 8, COLS)
            v = one_all[at, lax.rem(p, 8) // 2]
            chosen[s * 32 : s * 32 + 32] = jnp.where(lax.rem(p, 2) == 1, v[:, 64:], v[:, :64])
        wide = jnp.concatenate([c_one[n, s] for s in range(12)], axis=1)
        field[n] = mm(wide, chosen[0:384])
        return 0

    lax.fori_loop(0, 8, couple, 0, unroll=True)

    for copy in x_halo:
        copy.wait()
    for copy in corners:
        copy.start()

    def beside_x(i, _):
        prepare(1 + i, 0)
        prepare(1 + i, 5)
        return 0

    lax.fori_loop(0, 4, beside_x, 0, unroll=True)
    lax.fori_loop(8, 12, unit_step, 0)

    def wait_part(k, _):
        part_copy(k).wait()
        return 0

    lax.fori_loop(1, COLS, wait_part, 0)
    part = part_all[0]
    for k in range(1, COLS):
        part = part + part_all[k]
    top = jnp.concatenate([part[:, :64], part[:, 64:]], axis=0)
    top_high = top.astype(BF16)
    top_low = (top - top_high.astype(F32)).astype(BF16)

    def lower(n, _):
        rows = pl.ds(pl.multiple_of(n * 32, 32), 32)
        t = t_two[rows]
        one = field[n] + mm(t, top_high) + mm(t, top_low)
        high = one.astype(BF16)
        rest = (one - high.astype(F32)).astype(BF16)
        coef[n] = (mm(t_one[n], high) + mm(t_one[n], rest)).astype(BF16)
        return 0

    lax.fori_loop(0, 8, lower, 0, unroll=True)

    def finish(i, _):
        x1, y = i // 4, lax.rem(i, 4)
        even, odd = 2 * x1 * 4 + y, (2 * x1 + 1) * 4 + y
        for h in range(2):
            at = slice(h * 128, h * 128 + 128)
            a, b = near[even, :, at], near[odd, :, at]
            for z0 in range(2):
                tile = lax.rem(y, 2) + 2 * z0 + 4 * x1 + 8 * (y // 2) + 16 * h
                rows = pl.ds(pl.multiple_of(lax.rem(tile, 4) * 64, 64), 64)
                far = mm(coef[tile // 4, rows], split_basis[tile], TN)
                lanes = pl.ds(pl.multiple_of(tile * 128, 128), 128)
                out[:, lanes] = (halves(a, b, z0) * SCALE + far).astype(BF16)
        return 0

    for copy in corners:
        copy.wait()
    for y in (0, 5):
        for x in (0, 5):
            prepare(y, x)
    lax.fori_loop(12, 16, unit_step, 0)
    lax.fori_loop(0, 8, finish, 0, unroll=True)


def shards(charges, points, leaf_basis, transfer_one, transfer_two, couple_one, couple_two, near_list, list_one, list_two):
    vmem = pl.BlockSpec(memory_space=pltpu.VMEM)
    smem = pl.BlockSpec(memory_space=pltpu.SMEM)
    dma = pltpu.SemaphoreType.DMA
    return pl.pallas_call(
        body,
        out_shape=jax.ShapeDtypeStruct(charges.shape, BF16),
        in_specs=[vmem] * 8 + [smem, vmem, vmem],
        out_specs=vmem,
        scratch_shapes=[
            pltpu.VMEM((6, 6, 64, 256), BF16),
            pltpu.VMEM((6, 6, 4, 256), F32),
            pltpu.VMEM((36, 64, 512), BF16),
            pltpu.VMEM((36, 24, 128), F32),
            pltpu.VMEM((16, 4, 320, 128), F32),
            pltpu.VMEM((9, 128, 128), F32),
            pltpu.VMEM((2048, 32), F32),
            pltpu.VMEM((8, 256, 32), BF16),
            pltpu.VMEM((16, 64, 256), F32),
            pltpu.VMEM((32, 64, 128), BF16),
            pltpu.VMEM((8, 256, 64), BF16),
            pltpu.VMEM((9, 4, 32, 128), BF16),
            pltpu.VMEM((16, 128), BF16),
            pltpu.VMEM((33, 16, 128), BF16),
            pltpu.VMEM((8, 32, 512), BF16),
            pltpu.VMEM((8, 8, 128), jnp.int32),
            pltpu.SMEM((8, 8, 128), jnp.int32),
            pltpu.VMEM((512, 64), BF16),
            pltpu.VMEM((8, 32, 64), F32),
            pltpu.VMEM((8, 16, 128), F32),
            pltpu.VMEM((8, 16, 128), F32),
            dma((16,)),
            dma((16,)),
            dma((COLS,)),
            dma((COLS,)),
            dma((12,)),
            dma((12,)),
            dma((COLS,)),
            dma((COLS,)),
            dma((COLS,)),
            dma((COLS,)),
            dma((COLS,)),
            dma((COLS,)),
            dma,
        ],
        compiler_params=pltpu.CompilerParams(
            collective_id=0, has_side_effects=True, vmem_limit_bytes=58 * 2**20
        ),
    )(
        charges,
        points,
        leaf_basis,
        transfer_one.transpose(1, 2, 0).reshape(1024, 64),
        transfer_two.reshape(256, 32),
        couple_one,
        couple_two.reshape(16, 32, 32),
        near_list.T,
        list_one,
        list_two,
        jnp.asarray(picks(), BF16),
    )


def solution(mesh):
    lead = ("row", "col")
    columns, three = P(None, lead), P(lead, None, None)
    four, two = P(lead, None, None, None), P(lead, None)
    in_specs = (columns, columns, columns, three, three, four, four, two, two, two)
    return jax.shard_map(shards, mesh=mesh, in_specs=in_specs, out_specs=columns, check_vma=False)
```

```python
import jax
import jax.numpy as jnp
import numpy as np
from jax import lax
from jax.experimental import pallas as pl
from jax.experimental.pallas import tpu as pltpu
from jax.sharding import PartitionSpec as P

F32 = jnp.float32
BF16 = jnp.bfloat16
MESH = pl.DeviceIdType.MESH
NT = (((1,), (1,)), ((), ()))
TN = (((0,), (0,)), ((), ()))
NN = (((1,), (0,)), ((), ()))

ROWS = 32
COLS = 8
SOFT = 0.0025
SCALE = (27 * 64) ** (-0.5)


def mm(a, b, dims=NN):
    return lax.dot_general(a, b, dims, preferred_element_type=F32)


def picks():
    pick = np.zeros((256, 192), np.float32)
    sides = (((0, 1, 1, 2, 3), (0, -1, 1, 0, -1)), ((0, 1, 2, 2, 3), (1, 0, -1, 1, 0)))
    for side, (places, steps) in enumerate(sides):
        for x in range(4):
            for y in range(4):
                for tile in range(5):
                    z = places[tile]
                    leaf = x % 2 + 2 * (y % 2) + 4 * (z % 2) + 8 * (x // 2) + 16 * (y // 2) + 32 * (z // 2)
                    pick[side * 128 + (x * 4 + y) * 8 + tile, (steps[tile] + 1) * 64 + leaf] = 1
    return pick


def body(
    charges,
    points,
    basis,
    t_packed,
    t_two,
    c_one,
    c_two,
    near_list,
    list_one,
    list_two,
    pick,
    out,
    ext_c,
    ext_p,
    wide_c,
    src_f,
    own_f,
    masks,
    t_flat,
    t_one,
    near,
    split_basis,
    coef,
    one_all,
    two_send,
    two_all,
    ctwo_all,
    lists_all,
    lists_s,
    chosen,
    field,
    part_send,
    part_all,
    halo_s,
    halo_r,
    one_s,
    one_r,
    two_s,
    two_r,
    ctwo_s,
    ctwo_r,
    lt_s,
    lt_r,
    part_s,
    part_r,
    local,
):
    r = lax.axis_index("row")
    c = lax.axis_index("col")
    barrier = pltpu.get_barrier_semaphore()

    def greet_col(k, _):
        pl.semaphore_signal(barrier, inc=1, device_id=(r, lax.rem(c + k, COLS)), device_id_type=MESH)
        return 0

    layer, spot = r // 4, lax.rem(r, 4)

    def quad_peer(k):
        return (layer * 4 + lax.rem(spot + k, 4), c)

    def ring_peer(k):
        return (lax.rem(layer + k, 8) * 4 + spot, c)

    def greet_ring(k, _):
        pl.semaphore_signal(barrier, inc=1, device_id=ring_peer(k), device_id_type=MESH)
        return 0

    lax.fori_loop(1, COLS, greet_col, 0)
    lax.fori_loop(1, 8, greet_ring, 0)
    up, down = (lax.rem(r + 1, ROWS), c), (lax.rem(r + ROWS - 1, ROWS), c)
    for peer in (quad_peer(1), quad_peer(2), quad_peer(3), up, down):
        pl.semaphore_signal(barrier, inc=1, device_id=peer, device_id_type=MESH)

    low = lax.broadcasted_iota(jnp.int32, (64, 128), 1) < 64

    def halves(a, b, upper):
        if upper:
            return jnp.concatenate([a[:, 64:], b[:, 64:]], axis=1)
        return jnp.concatenate([a[:, :64], b[:, :64]], axis=1)

    def arrange(i, _):
        x1, y = i // 4, lax.rem(i, 4)
        for h in range(2):
            tile = lax.rem(y, 2) + 4 * x1 + 8 * (y // 2) + 16 * h
            first = pl.ds(pl.multiple_of(tile * 128, 128), 128)
            second = pl.ds(pl.multiple_of(tile * 128 + 256, 128), 128)
            at = slice(h * 128, h * 128 + 128)
            a, b = charges[:, first], charges[:, second]
            pa, pb = points[:, first], points[:, second]
            for x0 in range(2):
                ext_c[1 + y, 1 + 2 * x1 + x0, :, at] = halves(a, b, x0)
                ext_p[1 + y, 1 + 2 * x1 + x0, 0:3, at] = halves(pa, pb, x0)
                ext_p[1 + y, 1 + 2 * x1 + x0, 3:4, at] = jnp.zeros((1, 128), F32)
        return 0

    lax.fori_loop(0, 8, arrange, 0, unroll=True)

    ctwo_all[c] = jnp.concatenate([c_two[s] for s in range(16)], axis=1)
    lists_all[c] = jnp.zeros((8, 128), jnp.int32)
    lists_all[c, 0:1, 0:16] = list_two[...]

    def halo(n, ref, src, dst, device):
        return pltpu.make_async_remote_copy(
            src_ref=ref.at[src],
            dst_ref=ref.at[dst],
            send_sem=halo_s.at[n],
            recv_sem=halo_r.at[n],
            device_id=device,
            device_id_type=MESH,
        )

    right, left = (r, lax.rem(c + 1, COLS)), (r, lax.rem(c + COLS - 1, COLS))
    four = pl.ds(1, 4)
    x_halo, y_halo, corners = [], [], []
    for i, ref in enumerate((ext_c, ext_p)):
        x_halo.append(halo(8 * i + 0, ref, (four, 4), (four, 0), right))
        x_halo.append(halo(8 * i + 1, ref, (four, 1), (four, 5), left))
        y_halo.append(halo(8 * i + 2, ref, (4, four), (0, four), up))
        y_halo.append(halo(8 * i + 3, ref, (1, four), (5, four), down))
        corners.append(halo(8 * i + 4, ref, (4, 0), (0, 0), up))
        corners.append(halo(8 * i + 5, ref, (4, 5), (0, 5), up))
        corners.append(halo(8 * i + 6, ref, (1, 0), (5, 0), down))
        corners.append(halo(8 * i + 7, ref, (1, 5), (5, 5), down))

    def to_col(k, src, ref, send, recv):
        return pltpu.make_async_remote_copy(
            src_ref=src,
            dst_ref=ref.at[c],
            send_sem=send.at[k],
            recv_sem=recv.at[k],
            device_id=(r, lax.rem(c + k, COLS)),
            device_id_type=MESH,
        )

    def to_quad(k):
        return pltpu.make_async_remote_copy(
            src_ref=two_send,
            dst_ref=two_all.at[r],
            send_sem=two_s.at[k],
            recv_sem=two_r.at[k],
            device_id=quad_peer(k),
            device_id_type=MESH,
        )

    def to_ring(k):
        quad = two_all.at[pl.ds(layer * 4, 4)]
        return pltpu.make_async_remote_copy(
            src_ref=quad,
            dst_ref=quad,
            send_sem=two_s.at[4 + k],
            recv_sem=two_r.at[4 + k],
            device_id=ring_peer(k),
            device_id_type=MESH,
        )

    far_y = c + 1 - 2 * lax.rem(c, 2)
    place = c // 2

    def across(ref, send, recv):
        return pltpu.make_async_remote_copy(
            src_ref=ref.at[c],
            dst_ref=ref.at[c],
            send_sem=send.at[0],
            recv_sem=recv.at[0],
            device_id=(r, far_y),
            device_id_type=MESH,
        )

    def along(k, ref, send, recv):
        both = ref.at[pl.ds(place * 2, 2)]
        return pltpu.make_async_remote_copy(
            src_ref=both,
            dst_ref=both,
            send_sem=send.at[k],
            recv_sem=recv.at[k],
            device_id=(r, lax.rem(place + k, 4) * 2 + lax.rem(c, 2)),
            device_id_type=MESH,
        )

    gathers = ((ctwo_all, ctwo_s, ctwo_r), (lists_all, lt_s, lt_r), (one_all, one_s, one_r))

    for a in range(0, 32, 4):
        turned = jnp.transpose(t_packed[a * 32 : a * 32 + 128].astype(F32))
        for q in range(4):
            t_flat[pl.ds(a + q, 64, stride=32)] = turned[:, q * 32 : q * 32 + 32]
    for n in range(8):
        t_one[n] = t_flat[n * 256 : n * 256 + 256].astype(BF16)

    for tile in range(32):
        b = basis[:, tile * 128 : tile * 128 + 128]
        zero = jnp.zeros((32, 64), BF16)
        split_basis[tile] = jnp.concatenate(
            [jnp.concatenate([b[:, :64], zero], axis=1), jnp.concatenate([zero, b[:, 64:]], axis=1)], axis=0
        )

    def lift(n, _):
        for i in range(4):
            lanes = pl.ds(pl.multiple_of(n * 512 + i * 128, 128), 128)
            coef[n, i * 64 : i * 64 + 64] = mm(split_basis[n * 4 + i], charges[:, lanes], NT).astype(BF16)
        field[n] = mm(t_one[n], coef[n], TN)
        return 0

    lax.fori_loop(0, 8, lift, 0, unroll=True)
    ones = [field[n].astype(BF16) for n in range(8)]
    for i in range(4):
        one_all[c, i] = jnp.concatenate([ones[2 * i], ones[2 * i + 1]], axis=1)
    two = mm(t_two[...], jnp.concatenate(ones, axis=0), TN).astype(BF16)
    two_send[...] = jnp.concatenate([two[:16], two[16:]], axis=1)

    def start_ring(k, _):
        to_ring(k).start()
        return 0

    active = jnp.transpose(jnp.where(near_list[...] >= 0, 1.0, 0.0))
    lists = jnp.concatenate([active[:, 0:9], active[:, 9:18], active[:, 18:27]], axis=0).astype(BF16)
    blocked = jnp.where(mm(pick[...], lists) > 0.5, 0.0, jnp.inf)
    low2 = lax.broadcasted_iota(jnp.int32, (128, 128), 1) < 64
    for j in range(9):
        masks[j] = jnp.where(low2, blocked[0:128, j : j + 1], blocked[128:256, j : j + 1])

    pl.semaphore_wait(barrier, COLS - 1 + 7 + 5)
    for k in (1, 2, 3):
        to_quad(k).start()
    for gather in gathers:
        across(*gather).start()
    for copy in y_halo:
        copy.start()
    one_all[COLS] = jnp.zeros((4, 32, 128), BF16)
    two_all[r] = two_send[...]
    two_all[ROWS] = jnp.zeros((16, 128), BF16)

    coord = lax.broadcasted_iota(jnp.int32, (4, 256), 0)
    middle = jnp.where(coord == 0, 4 * c + 2, jnp.where(coord == 1, 4 * r + 2, jnp.where(coord == 2, 2, 0))).astype(F32)

    def prepare(y, x):
        p = ext_p[y, x] - middle
        q = p * p
        size = q[0:1] + q[1:2] + q[2:3]
        f = jnp.concatenate([-2.0 * p[0:3], size, jnp.zeros((4, 256), F32)], axis=0)
        e = y * 6 + x
        f0, f1 = f[:, :128], f[:, 128:]
        src_f[e, 0:8] = f0
        src_f[e, 8:16] = jnp.where(low[:8], f1, f0)
        src_f[e, 16:24] = f1
        ch = ext_c[y, x]
        c0, c1 = ch[:, :128], ch[:, 128:]
        zero = jnp.zeros((64, 64), BF16)
        wide_c[e, :, 0:128] = c0
        wide_c[e, :, 128:256] = jnp.concatenate([c1[:, :64], zero], axis=1)
        wide_c[e, :, 256:384] = c1
        wide_c[e, :, 384:512] = jnp.concatenate([zero, c0[:, 64:]], axis=1)
        return p, size

    at_row = lax.rem(lax.broadcasted_iota(jnp.int32, (32, 512), 0), 8)
    at_lane = lax.broadcasted_iota(jnp.int32, (32, 512), 1) // 128
    spread = jnp.where(at_row == at_lane, 1.0, 0.0).astype(BF16)

    def own_column(i, _):
        x, y = i // 4, lax.rem(i, 4)
        p, size = prepare(1 + y, 1 + x)
        whole = jnp.concatenate([p[0:3], size + SOFT, jnp.zeros((4, 256), F32)], axis=0)
        first = whole.astype(BF16).astype(F32)
        rest = whole - first
        second = rest.astype(BF16).astype(F32)
        parts = jnp.concatenate([first, second, rest - second, jnp.zeros((8, 256), F32)], axis=0).astype(BF16)
        wide = mm(parts, spread, TN)
        for f in range(4):
            w = wide[:, f * 128 : f * 128 + 128]
            own_f[i, f, 0:256] = w
            own_f[i, f, 256:320] = jnp.where(low, w[64:128], w[128:192])
        return 0

    lax.fori_loop(0, 16, own_column, 0, unroll=2)

    def unit(i):
        g, k = i // 4, lax.rem(i, 4)
        gx, gy, a, b = g // 2, lax.rem(g, 2), k // 2, lax.rem(k, 2)
        x = (1 - gx) * (1 + a) + gx * 3 * a
        y = (1 - gy) * (1 + b) + gy * 3 * b
        d = x * 4 + y
        total = [jnp.zeros((128, 64), F32), jnp.zeros((128, 64), F32)]
        zero = jnp.zeros((64, 128), BF16)
        for j in range(9):
            e = (y + j // 3) * 6 + x + j % 3
            rows = pl.ds(pl.multiple_of(d * 8, 8), 8)
            s0, sm, s1 = src_f[e, 0:8], src_f[e, 8:16], src_f[e, 16:24]
            m = masks[j, rows]

            def tile(t, first, s):
                dist = own_f[d, 3, first : first + 64] + (s[3:4] + m[t : t + 1])
                for f in range(3):
                    dist = dist + own_f[d, f, first : first + 64] * s[f : f + 1]
                return lax.rsqrt(dist.astype(BF16))

            mid = tile(2, 256, sm)
            k0 = jnp.concatenate(
                [jnp.concatenate([tile(0, 0, s0), zero], 1), jnp.concatenate([tile(1, 64, s0), mid], 1)], 0
            )
            k1 = jnp.concatenate(
                [jnp.concatenate([tile(3, 128, s1), mid], 1), jnp.concatenate([tile(4, 192, s1), zero], 1)], 0
            )
            total[0] = total[0] + mm(k0, wide_c[e, :, 0:256], NT)
            total[1] = total[1] + mm(k1, wide_c[e, :, 256:512], NT)
        near[d, :, 0:128] = jnp.transpose(total[0])
        near[d, :, 128:256] = jnp.transpose(total[1])

    def unit_step(i, _):
        unit(i)
        return 0

    for k in (1, 2, 3):
        to_quad(k).wait()
    lax.fori_loop(1, 8, start_ring, 0)
    for gather in gathers:
        across(*gather).wait()
        for k in (1, 2, 3):
            along(k, *gather).start()
    for copy in x_halo:
        copy.start()
    lax.fori_loop(0, 4, unit_step, 0, unroll=4)

    for copy in y_halo:
        copy.wait()

    def beside_y(i, _):
        prepare(0, 1 + i)
        prepare(5, 1 + i)
        return 0

    lax.fori_loop(0, 4, beside_y, 0, unroll=True)
    lax.fori_loop(4, 8, unit_step, 0, unroll=4)

    def wait_ring(k, _):
        to_ring(k).wait()
        return 0

    for gather in gathers[:2]:
        for k in (1, 2, 3):
            along(k, *gather).wait()
    to_scalar = pltpu.make_async_copy(lists_all, lists_s, local)
    to_scalar.start()
    to_scalar.wait()
    lax.fori_loop(1, 8, wait_ring, 0)

    def share(k, _):
        peer = lax.rem(c + k, COLS)
        for s in range(16):
            node = lists_s[peer, 0, s]
            at = jnp.where(lax.rem(node, COLS) == c, node // COLS, ROWS)
            v = two_all[at]
            chosen[s * 32 : s * 32 + 16] = v[:, :64]
            chosen[s * 32 + 16 : s * 32 + 32] = v[:, 64:]
        part = mm(ctwo_all[peer], chosen[...])
        part_send[k] = jnp.concatenate([part[:16], part[16:]], axis=1)
        return 0

    def part_copy(k):
        return to_col(k, part_send.at[k], part_all, part_s, part_r)

    def share_and_send(k, _):
        share(k, 0)
        part_copy(k).start()
        return 0

    lax.fori_loop(1, COLS, share_and_send, 0, unroll=True)
    share(0, 0)
    part_all[c] = part_send[0]

    for k in (1, 2, 3):
        along(k, *gathers[2]).wait()
    start = r * 64

    def couple(n, _):
        for s in range(12):
            node = list_one[n, s]
            p = jnp.clip(node - start, 0, 63)
            at = jnp.where(node >= 0, p // 8, COLS)
            v = one_all[at, lax.rem(p, 8) // 2]
            chosen[s * 32 : s * 32 + 32] = jnp.where(lax.rem(p, 2) == 1, v[:, 64:], v[:, :64])
        wide = jnp.concatenate([c_one[n, s] for s in range(12)], axis=1)
        field[n] = mm(wide, chosen[0:384])
        return 0

    lax.fori_loop(0, 8, couple, 0, unroll=True)

    for copy in x_halo:
        copy.wait()
    for copy in corners:
        copy.start()

    def beside_x(i, _):
        prepare(1 + i, 0)
        prepare(1 + i, 5)
        return 0

    lax.fori_loop(0, 4, beside_x, 0, unroll=True)
    lax.fori_loop(8, 12, unit_step, 0, unroll=4)

    def wait_part(k, _):
        part_copy(k).wait()
        return 0

    lax.fori_loop(1, COLS, wait_part, 0)
    part = part_all[0]
    for k in range(1, COLS):
        part = part + part_all[k]
    top = jnp.concatenate([part[:, :64], part[:, 64:]], axis=0)
    top_high = top.astype(BF16)
    top_low = (top - top_high.astype(F32)).astype(BF16)

    def lower(n, _):
        rows = pl.ds(pl.multiple_of(n * 32, 32), 32)
        t = t_two[rows]
        one = field[n] + mm(t, top_high) + mm(t, top_low)
        high = one.astype(BF16)
        rest = (one - high.astype(F32)).astype(BF16)
        coef[n] = (mm(t_one[n], high) + mm(t_one[n], rest)).astype(BF16)
        return 0

    lax.fori_loop(0, 8, lower, 0, unroll=True)

    def finish(i, _):
        x1, y = i // 4, lax.rem(i, 4)
        even, odd = 2 * x1 * 4 + y, (2 * x1 + 1) * 4 + y
        for h in range(2):
            at = slice(h * 128, h * 128 + 128)
            a, b = near[even, :, at], near[odd, :, at]
            for z0 in range(2):
                tile = lax.rem(y, 2) + 2 * z0 + 4 * x1 + 8 * (y // 2) + 16 * h
                rows = pl.ds(pl.multiple_of(lax.rem(tile, 4) * 64, 64), 64)
                far = mm(coef[tile // 4, rows], split_basis[tile], TN)
                lanes = pl.ds(pl.multiple_of(tile * 128, 128), 128)
                out[:, lanes] = (halves(a, b, z0) * SCALE + far).astype(BF16)
        return 0

    for copy in corners:
        copy.wait()
    for y in (0, 5):
        for x in (0, 5):
            prepare(y, x)
    lax.fori_loop(12, 16, unit_step, 0, unroll=4)
    lax.fori_loop(0, 8, finish, 0, unroll=True)


def shards(charges, points, leaf_basis, transfer_one, transfer_two, couple_one, couple_two, near_list, list_one, list_two):
    vmem = pl.BlockSpec(memory_space=pltpu.VMEM)
    smem = pl.BlockSpec(memory_space=pltpu.SMEM)
    dma = pltpu.SemaphoreType.DMA
    return pl.pallas_call(
        body,
        out_shape=jax.ShapeDtypeStruct(charges.shape, BF16),
        in_specs=[vmem] * 8 + [smem, vmem, vmem],
        out_specs=vmem,
        scratch_shapes=[
            pltpu.VMEM((6, 6, 64, 256), BF16),
            pltpu.VMEM((6, 6, 4, 256), F32),
            pltpu.VMEM((36, 64, 512), BF16),
            pltpu.VMEM((36, 24, 128), F32),
            pltpu.VMEM((16, 4, 320, 128), F32),
            pltpu.VMEM((9, 128, 128), F32),
            pltpu.VMEM((2048, 32), F32),
            pltpu.VMEM((8, 256, 32), BF16),
            pltpu.VMEM((16, 64, 256), F32),
            pltpu.VMEM((32, 64, 128), BF16),
            pltpu.VMEM((8, 256, 64), BF16),
            pltpu.VMEM((9, 4, 32, 128), BF16),
            pltpu.VMEM((16, 128), BF16),
            pltpu.VMEM((33, 16, 128), BF16),
            pltpu.VMEM((8, 32, 512), BF16),
            pltpu.VMEM((8, 8, 128), jnp.int32),
            pltpu.SMEM((8, 8, 128), jnp.int32),
            pltpu.VMEM((512, 64), BF16),
            pltpu.VMEM((8, 32, 64), F32),
            pltpu.VMEM((8, 16, 128), F32),
            pltpu.VMEM((8, 16, 128), F32),
            dma((16,)),
            dma((16,)),
            dma((COLS,)),
            dma((COLS,)),
            dma((12,)),
            dma((12,)),
            dma((COLS,)),
            dma((COLS,)),
            dma((COLS,)),
            dma((COLS,)),
            dma((COLS,)),
            dma((COLS,)),
            dma,
        ],
        compiler_params=pltpu.CompilerParams(
            collective_id=0, has_side_effects=True, vmem_limit_bytes=58 * 2**20
        ),
    )(
        charges,
        points,
        leaf_basis,
        transfer_one.transpose(1, 2, 0).reshape(1024, 64),
        transfer_two.reshape(256, 32),
        couple_one,
        couple_two.reshape(16, 32, 32),
        near_list.T,
        list_one,
        list_two,
        jnp.asarray(picks(), BF16),
    )


def solution(mesh):
    lead = ("row", "col")
    columns, three = P(None, lead), P(lead, None, None)
    four, two = P(lead, None, None, None), P(lead, None)
    in_specs = (columns, columns, columns, three, three, four, four, two, two, two)
    return jax.shard_map(shards, mesh=mesh, in_specs=in_specs, out_specs=columns, check_vma=False)
```

```python
import jax
import jax.numpy as jnp
import numpy as np
from jax import lax
from jax.experimental import pallas as pl
from jax.experimental.pallas import tpu as pltpu
from jax.sharding import PartitionSpec as P

F32 = jnp.float32
BF16 = jnp.bfloat16
MESH = pl.DeviceIdType.MESH
NT = (((1,), (1,)), ((), ()))
TN = (((0,), (0,)), ((), ()))
NN = (((1,), (0,)), ((), ()))

ROWS = 32
COLS = 8
SOFT = 0.0025
SCALE = (27 * 64) ** (-0.5)


def mm(a, b, dims=NN):
    return lax.dot_general(a, b, dims, preferred_element_type=F32)


def picks():
    pick = np.zeros((256, 192), np.float32)
    sides = (((0, 1, 1, 2, 3), (0, -1, 1, 0, -1)), ((0, 1, 2, 2, 3), (1, 0, -1, 1, 0)))
    for side, (places, steps) in enumerate(sides):
        for x in range(4):
            for y in range(4):
                for tile in range(5):
                    z = places[tile]
                    leaf = x % 2 + 2 * (y % 2) + 4 * (z % 2) + 8 * (x // 2) + 16 * (y // 2) + 32 * (z // 2)
                    pick[side * 128 + (x * 4 + y) * 8 + tile, (steps[tile] + 1) * 64 + leaf] = 1
    return pick


def body(
    charges,
    points,
    basis,
    t_packed,
    t_two,
    c_one,
    c_two,
    near_list,
    list_one,
    list_two,
    pick,
    out,
    ext_c,
    ext_p,
    wide_c,
    src_f,
    own_f,
    masks,
    t_flat,
    t_one,
    near,
    split_basis,
    coef,
    one_all,
    two_send,
    two_all,
    ctwo_all,
    lists_all,
    lists_s,
    chosen,
    field,
    part_send,
    part_all,
    halo_s,
    halo_r,
    one_s,
    one_r,
    two_s,
    two_r,
    ctwo_s,
    ctwo_r,
    lt_s,
    lt_r,
    part_s,
    part_r,
    local,
):
    r = lax.axis_index("row")
    c = lax.axis_index("col")
    barrier = pltpu.get_barrier_semaphore()

    def greet_col(k, _):
        pl.semaphore_signal(barrier, inc=1, device_id=(r, lax.rem(c + k, COLS)), device_id_type=MESH)
        return 0

    layer, spot = r // 4, lax.rem(r, 4)

    def quad_peer(k):
        return (layer * 4 + lax.rem(spot + k, 4), c)

    def ring_peer(k):
        return (lax.rem(layer + k, 8) * 4 + spot, c)

    def greet_ring(k, _):
        pl.semaphore_signal(barrier, inc=1, device_id=ring_peer(k), device_id_type=MESH)
        return 0

    lax.fori_loop(1, COLS, greet_col, 0)
    lax.fori_loop(1, 8, greet_ring, 0)
    up, down = (lax.rem(r + 1, ROWS), c), (lax.rem(r + ROWS - 1, ROWS), c)
    for peer in (quad_peer(1), quad_peer(2), quad_peer(3), up, down):
        pl.semaphore_signal(barrier, inc=1, device_id=peer, device_id_type=MESH)

    low = lax.broadcasted_iota(jnp.int32, (64, 128), 1) < 64

    def halves(a, b, upper):
        if upper:
            return jnp.concatenate([a[:, 64:], b[:, 64:]], axis=1)
        return jnp.concatenate([a[:, :64], b[:, :64]], axis=1)

    def arrange(i, _):
        x1, y = i // 4, lax.rem(i, 4)
        for h in range(2):
            tile = lax.rem(y, 2) + 4 * x1 + 8 * (y // 2) + 16 * h
            first = pl.ds(pl.multiple_of(tile * 128, 128), 128)
            second = pl.ds(pl.multiple_of(tile * 128 + 256, 128), 128)
            at = slice(h * 128, h * 128 + 128)
            a, b = charges[:, first], charges[:, second]
            pa, pb = points[:, first], points[:, second]
            for x0 in range(2):
                ext_c[1 + y, 1 + 2 * x1 + x0, :, at] = halves(a, b, x0)
                ext_p[1 + y, 1 + 2 * x1 + x0, 0:3, at] = halves(pa, pb, x0)
                ext_p[1 + y, 1 + 2 * x1 + x0, 3:4, at] = jnp.zeros((1, 128), F32)
        return 0

    lax.fori_loop(0, 8, arrange, 0, unroll=True)

    ctwo_all[c] = jnp.concatenate([c_two[s] for s in range(16)], axis=1)
    lists_all[c] = jnp.zeros((8, 128), jnp.int32)
    lists_all[c, 0:1, 0:16] = list_two[...]

    def halo(n, ref, src, dst, device):
        return pltpu.make_async_remote_copy(
            src_ref=ref.at[src],
            dst_ref=ref.at[dst],
            send_sem=halo_s.at[n],
            recv_sem=halo_r.at[n],
            device_id=device,
            device_id_type=MESH,
        )

    right, left = (r, lax.rem(c + 1, COLS)), (r, lax.rem(c + COLS - 1, COLS))
    four = pl.ds(1, 4)
    x_halo, y_halo, corners = [], [], []
    for i, ref in enumerate((ext_c, ext_p)):
        x_halo.append(halo(8 * i + 0, ref, (four, 4), (four, 0), right))
        x_halo.append(halo(8 * i + 1, ref, (four, 1), (four, 5), left))
        y_halo.append(halo(8 * i + 2, ref, (4, four), (0, four), up))
        y_halo.append(halo(8 * i + 3, ref, (1, four), (5, four), down))
        corners.append(halo(8 * i + 4, ref, (4, 0), (0, 0), up))
        corners.append(halo(8 * i + 5, ref, (4, 5), (0, 5), up))
        corners.append(halo(8 * i + 6, ref, (1, 0), (5, 0), down))
        corners.append(halo(8 * i + 7, ref, (1, 5), (5, 5), down))

    def to_col(k, src, ref, send, recv):
        return pltpu.make_async_remote_copy(
            src_ref=src,
            dst_ref=ref.at[c],
            send_sem=send.at[k],
            recv_sem=recv.at[k],
            device_id=(r, lax.rem(c + k, COLS)),
            device_id_type=MESH,
        )

    def to_quad(k):
        return pltpu.make_async_remote_copy(
            src_ref=two_send,
            dst_ref=two_all.at[r],
            send_sem=two_s.at[k],
            recv_sem=two_r.at[k],
            device_id=quad_peer(k),
            device_id_type=MESH,
        )

    def to_ring(k):
        quad = two_all.at[pl.ds(layer * 4, 4)]
        return pltpu.make_async_remote_copy(
            src_ref=quad,
            dst_ref=quad,
            send_sem=two_s.at[4 + k],
            recv_sem=two_r.at[4 + k],
            device_id=ring_peer(k),
            device_id_type=MESH,
        )

    far_y = c + 1 - 2 * lax.rem(c, 2)
    place = c // 2

    def across(ref, send, recv):
        return pltpu.make_async_remote_copy(
            src_ref=ref.at[c],
            dst_ref=ref.at[c],
            send_sem=send.at[0],
            recv_sem=recv.at[0],
            device_id=(r, far_y),
            device_id_type=MESH,
        )

    def along(k, ref, send, recv):
        both = ref.at[pl.ds(place * 2, 2)]
        return pltpu.make_async_remote_copy(
            src_ref=both,
            dst_ref=both,
            send_sem=send.at[k],
            recv_sem=recv.at[k],
            device_id=(r, lax.rem(place + k, 4) * 2 + lax.rem(c, 2)),
            device_id_type=MESH,
        )

    gathers = ((ctwo_all, ctwo_s, ctwo_r), (lists_all, lt_s, lt_r), (one_all, one_s, one_r))

    for a in range(0, 32, 4):
        turned = jnp.transpose(t_packed[a * 32 : a * 32 + 128].astype(F32))
        for q in range(4):
            t_flat[pl.ds(a + q, 64, stride=32)] = turned[:, q * 32 : q * 32 + 32]
    for n in range(8):
        t_one[n] = t_flat[n * 256 : n * 256 + 256].astype(BF16)

    for tile in range(32):
        b = basis[:, tile * 128 : tile * 128 + 128]
        zero = jnp.zeros((32, 64), BF16)
        split_basis[tile] = jnp.concatenate(
            [jnp.concatenate([b[:, :64], zero], axis=1), jnp.concatenate([zero, b[:, 64:]], axis=1)], axis=0
        )

    def lift(n, _):
        for i in range(4):
            lanes = pl.ds(pl.multiple_of(n * 512 + i * 128, 128), 128)
            coef[n, i * 64 : i * 64 + 64] = mm(split_basis[n * 4 + i], charges[:, lanes], NT).astype(BF16)
        field[n] = mm(t_one[n], coef[n], TN)
        return 0

    lax.fori_loop(0, 8, lift, 0, unroll=True)
    ones = [field[n].astype(BF16) for n in range(8)]
    for i in range(4):
        one_all[c, i] = jnp.concatenate([ones[2 * i], ones[2 * i + 1]], axis=1)
    two = mm(t_two[...], jnp.concatenate(ones, axis=0), TN).astype(BF16)
    two_send[...] = jnp.concatenate([two[:16], two[16:]], axis=1)

    def start_ring(k, _):
        to_ring(k).start()
        return 0

    active = jnp.transpose(jnp.where(near_list[...] >= 0, 1.0, 0.0))
    lists = jnp.concatenate([active[:, 0:9], active[:, 9:18], active[:, 18:27]], axis=0).astype(BF16)
    blocked = jnp.where(mm(pick[...], lists) > 0.5, 0.0, jnp.inf)
    low2 = lax.broadcasted_iota(jnp.int32, (128, 128), 1) < 64
    for j in range(9):
        masks[j] = jnp.where(low2, blocked[0:128, j : j + 1], blocked[128:256, j : j + 1])

    pl.semaphore_wait(barrier, COLS - 1 + 7 + 5)
    for k in (1, 2, 3):
        to_quad(k).start()
    for gather in gathers:
        across(*gather).start()
    for copy in y_halo:
        copy.start()
    one_all[COLS] = jnp.zeros((4, 32, 128), BF16)
    two_all[r] = two_send[...]
    two_all[ROWS] = jnp.zeros((16, 128), BF16)

    coord = lax.broadcasted_iota(jnp.int32, (4, 256), 0)
    middle = jnp.where(coord == 0, 4 * c + 2, jnp.where(coord == 1, 4 * r + 2, jnp.where(coord == 2, 2, 0))).astype(F32)

    def prepare(y, x):
        p = ext_p[y, x] - middle
        q = p * p
        size = q[0:1] + q[1:2] + q[2:3]
        f = jnp.concatenate([-2.0 * p[0:3], size, jnp.zeros((4, 256), F32)], axis=0)
        e = y * 6 + x
        f0, f1 = f[:, :128], f[:, 128:]
        src_f[e, 0:8] = f0
        src_f[e, 8:16] = jnp.where(low[:8], f1, f0)
        src_f[e, 16:24] = f1
        ch = ext_c[y, x]
        c0, c1 = ch[:, :128], ch[:, 128:]
        zero = jnp.zeros((64, 64), BF16)
        wide_c[e, :, 0:128] = c0
        wide_c[e, :, 128:256] = jnp.concatenate([c1[:, :64], zero], axis=1)
        wide_c[e, :, 256:384] = c1
        wide_c[e, :, 384:512] = jnp.concatenate([zero, c0[:, 64:]], axis=1)
        return p, size

    at_row = lax.rem(lax.broadcasted_iota(jnp.int32, (32, 512), 0), 8)
    at_lane = lax.broadcasted_iota(jnp.int32, (32, 512), 1) // 128
    spread = jnp.where(at_row == at_lane, 1.0, 0.0).astype(BF16)

    def own_column(i, _):
        x, y = i // 4, lax.rem(i, 4)
        p, size = prepare(1 + y, 1 + x)
        whole = jnp.concatenate([p[0:3], size + SOFT, jnp.zeros((4, 256), F32)], axis=0)
        first = whole.astype(BF16).astype(F32)
        rest = whole - first
        second = rest.astype(BF16).astype(F32)
        parts = jnp.concatenate([first, second, rest - second, jnp.zeros((8, 256), F32)], axis=0).astype(BF16)
        wide = mm(parts, spread, TN)
        for f in range(4):
            w = wide[:, f * 128 : f * 128 + 128]
            own_f[i, f, 0:256] = w
            own_f[i, f, 256:320] = jnp.where(low, w[64:128], w[128:192])
        return 0

    lax.fori_loop(0, 16, own_column, 0, unroll=2)

    def unit(i):
        g, k = i // 4, lax.rem(i, 4)
        gx, gy, a, b = g // 2, lax.rem(g, 2), k // 2, lax.rem(k, 2)
        x = (1 - gx) * (1 + a) + gx * 3 * a
        y = (1 - gy) * (1 + b) + gy * 3 * b
        d = x * 4 + y
        total = [jnp.zeros((128, 64), F32), jnp.zeros((128, 64), F32)]
        zero = jnp.zeros((64, 128), BF16)
        for j in range(9):
            e = (y + j // 3) * 6 + x + j % 3
            rows = pl.ds(pl.multiple_of(d * 8, 8), 8)
            s0, sm, s1 = src_f[e, 0:8], src_f[e, 8:16], src_f[e, 16:24]
            m = masks[j, rows]

            def tile(t, first, s):
                dist = own_f[d, 3, first : first + 64] + (s[3:4] + m[t : t + 1])
                for f in range(3):
                    dist = dist + own_f[d, f, first : first + 64] * s[f : f + 1]
                return lax.rsqrt(dist.astype(BF16))

            mid = tile(2, 256, sm)
            k0 = jnp.concatenate(
                [jnp.concatenate([tile(0, 0, s0), zero], 1), jnp.concatenate([tile(1, 64, s0), mid], 1)], 0
            )
            k1 = jnp.concatenate(
                [jnp.concatenate([tile(3, 128, s1), mid], 1), jnp.concatenate([tile(4, 192, s1), zero], 1)], 0
            )
            total[0] = total[0] + mm(k0, wide_c[e, :, 0:256], NT)
            total[1] = total[1] + mm(k1, wide_c[e, :, 256:512], NT)
        near[d, :, 0:128] = jnp.transpose(total[0])
        near[d, :, 128:256] = jnp.transpose(total[1])

    def unit_step(i, _):
        unit(i)
        return 0

    for copy in x_halo:
        copy.start()
    for k in (1, 2, 3):
        to_quad(k).wait()
    lax.fori_loop(1, 8, start_ring, 0)
    for gather in gathers:
        across(*gather).wait()
        for k in (1, 2, 3):
            along(k, *gather).start()
    lax.fori_loop(0, 4, unit_step, 0, unroll=4)

    for copy in y_halo:
        copy.wait()

    def beside_y(i, _):
        prepare(0, 1 + i)
        prepare(5, 1 + i)
        return 0

    lax.fori_loop(0, 4, beside_y, 0, unroll=True)
    lax.fori_loop(4, 8, unit_step, 0, unroll=4)

    def wait_ring(k, _):
        to_ring(k).wait()
        return 0

    for gather in gathers[:2]:
        for k in (1, 2, 3):
            along(k, *gather).wait()
    to_scalar = pltpu.make_async_copy(lists_all, lists_s, local)
    to_scalar.start()
    to_scalar.wait()
    lax.fori_loop(1, 8, wait_ring, 0)

    def share(k, _):
        peer = lax.rem(c + k, COLS)
        for s in range(16):
            node = lists_s[peer, 0, s]
            at = jnp.where(lax.rem(node, COLS) == c, node // COLS, ROWS)
            v = two_all[at]
            chosen[s * 32 : s * 32 + 16] = v[:, :64]
            chosen[s * 32 + 16 : s * 32 + 32] = v[:, 64:]
        part = mm(ctwo_all[peer], chosen[...])
        part_send[k] = jnp.concatenate([part[:16], part[16:]], axis=1)
        return 0

    def part_copy(k):
        return to_col(k, part_send.at[k], part_all, part_s, part_r)

    def share_and_send(k, _):
        share(k, 0)
        part_copy(k).start()
        return 0

    lax.fori_loop(1, COLS, share_and_send, 0, unroll=True)
    share(0, 0)
    part_all[c] = part_send[0]

    for k in (1, 2, 3):
        along(k, *gathers[2]).wait()
    start = r * 64

    def couple(n, _):
        for s in range(12):
            node = list_one[n, s]
            p = jnp.clip(node - start, 0, 63)
            at = jnp.where(node >= 0, p // 8, COLS)
            v = one_all[at, lax.rem(p, 8) // 2]
            chosen[s * 32 : s * 32 + 32] = jnp.where(lax.rem(p, 2) == 1, v[:, 64:], v[:, :64])
        wide = jnp.concatenate([c_one[n, s] for s in range(12)], axis=1)
        field[n] = mm(wide, chosen[0:384])
        return 0

    lax.fori_loop(0, 8, couple, 0, unroll=True)

    for copy in x_halo:
        copy.wait()
    for copy in corners:
        copy.start()

    def beside_x(i, _):
        prepare(1 + i, 0)
        prepare(1 + i, 5)
        return 0

    lax.fori_loop(0, 4, beside_x, 0, unroll=True)
    lax.fori_loop(8, 12, unit_step, 0, unroll=4)

    def wait_part(k, _):
        part_copy(k).wait()
        return 0

    lax.fori_loop(1, COLS, wait_part, 0)
    part = part_all[0]
    for k in range(1, COLS):
        part = part + part_all[k]
    top = jnp.concatenate([part[:, :64], part[:, 64:]], axis=0)
    top_high = top.astype(BF16)
    top_low = (top - top_high.astype(F32)).astype(BF16)

    def lower(n, _):
        rows = pl.ds(pl.multiple_of(n * 32, 32), 32)
        t = t_two[rows]
        one = field[n] + mm(t, top_high) + mm(t, top_low)
        high = one.astype(BF16)
        rest = (one - high.astype(F32)).astype(BF16)
        coef[n] = (mm(t_one[n], high) + mm(t_one[n], rest)).astype(BF16)
        return 0

    lax.fori_loop(0, 8, lower, 0, unroll=True)

    def finish(i, _):
        x1, y = i // 4, lax.rem(i, 4)
        even, odd = 2 * x1 * 4 + y, (2 * x1 + 1) * 4 + y
        for h in range(2):
            at = slice(h * 128, h * 128 + 128)
            a, b = near[even, :, at], near[odd, :, at]
            for z0 in range(2):
                tile = lax.rem(y, 2) + 2 * z0 + 4 * x1 + 8 * (y // 2) + 16 * h
                rows = pl.ds(pl.multiple_of(lax.rem(tile, 4) * 64, 64), 64)
                far = mm(coef[tile // 4, rows], split_basis[tile], TN)
                lanes = pl.ds(pl.multiple_of(tile * 128, 128), 128)
                out[:, lanes] = (halves(a, b, z0) * SCALE + far).astype(BF16)
        return 0

    for copy in corners:
        copy.wait()
    for y in (0, 5):
        for x in (0, 5):
            prepare(y, x)
    lax.fori_loop(12, 16, unit_step, 0, unroll=4)
    lax.fori_loop(0, 8, finish, 0, unroll=True)


def shards(charges, points, leaf_basis, transfer_one, transfer_two, couple_one, couple_two, near_list, list_one, list_two):
    vmem = pl.BlockSpec(memory_space=pltpu.VMEM)
    smem = pl.BlockSpec(memory_space=pltpu.SMEM)
    dma = pltpu.SemaphoreType.DMA
    return pl.pallas_call(
        body,
        out_shape=jax.ShapeDtypeStruct(charges.shape, BF16),
        in_specs=[vmem] * 8 + [smem, vmem, vmem],
        out_specs=vmem,
        scratch_shapes=[
            pltpu.VMEM((6, 6, 64, 256), BF16),
            pltpu.VMEM((6, 6, 4, 256), F32),
            pltpu.VMEM((36, 64, 512), BF16),
            pltpu.VMEM((36, 24, 128), F32),
            pltpu.VMEM((16, 4, 320, 128), F32),
            pltpu.VMEM((9, 128, 128), F32),
            pltpu.VMEM((2048, 32), F32),
            pltpu.VMEM((8, 256, 32), BF16),
            pltpu.VMEM((16, 64, 256), F32),
            pltpu.VMEM((32, 64, 128), BF16),
            pltpu.VMEM((8, 256, 64), BF16),
            pltpu.VMEM((9, 4, 32, 128), BF16),
            pltpu.VMEM((16, 128), BF16),
            pltpu.VMEM((33, 16, 128), BF16),
            pltpu.VMEM((8, 32, 512), BF16),
            pltpu.VMEM((8, 8, 128), jnp.int32),
            pltpu.SMEM((8, 8, 128), jnp.int32),
            pltpu.VMEM((512, 64), BF16),
            pltpu.VMEM((8, 32, 64), F32),
            pltpu.VMEM((8, 16, 128), F32),
            pltpu.VMEM((8, 16, 128), F32),
            dma((16,)),
            dma((16,)),
            dma((COLS,)),
            dma((COLS,)),
            dma((12,)),
            dma((12,)),
            dma((COLS,)),
            dma((COLS,)),
            dma((COLS,)),
            dma((COLS,)),
            dma((COLS,)),
            dma((COLS,)),
            dma,
        ],
        compiler_params=pltpu.CompilerParams(
            collective_id=0, has_side_effects=True, vmem_limit_bytes=58 * 2**20
        ),
    )(
        charges,
        points,
        leaf_basis,
        transfer_one.transpose(1, 2, 0).reshape(1024, 64),
        transfer_two.reshape(256, 32),
        couple_one,
        couple_two.reshape(16, 32, 32),
        near_list.T,
        list_one,
        list_two,
        jnp.asarray(picks(), BF16),
    )


def solution(mesh):
    lead = ("row", "col")
    columns, three = P(None, lead), P(lead, None, None)
    four, two = P(lead, None, None, None), P(lead, None)
    in_specs = (columns, columns, columns, three, three, four, four, two, two, two)
    return jax.shard_map(shards, mesh=mesh, in_specs=in_specs, out_specs=columns, check_vma=False)
```
